512 devices in a mesh: gx: 16 (over x_hi, y), gy: 16 (over z, x_lo), dev: 2 (over core).
Axes of the slice: x: 4 (x_hi: 2, x_lo: 2; x = x_hi * 2 + x_lo), y: 8, z: 8, core: 2. Of those that a mesh axis runs over, the one named last changes fastest.
Arguments:
- fine_now: float32 [3, 8, 256, 4096], P(None, 'dev', 'gx', 'gy'), may hold values from -6 to 6
- fine_before: float32 [3, 8, 256, 4096], P(None, 'dev', 'gx', 'gy'), may hold values from -6 to 6
- fine_material: float32 [4, 8, 256, 4096], P(None, 'dev', 'gx', 'gy'), may hold values from 0.5 to 2
- coarse_now: float32 [3, 16, 128, 2048], P(None, 'dev', 'gx', 'gy'), may hold values from -6 to 6
- coarse_before: float32 [3, 16, 128, 2048], P(None, 'dev', 'gx', 'gy'), may hold values from -6 to 6
- coarse_material: float32 [3, 16, 128, 2048], P(None, 'dev', 'gx', 'gy'), may hold values from 0.5 to 2
Outputs:
- fine_after: float32 [3, 8, 256, 4096], P(None, 'dev', 'gx', 'gy')
- coarse_after: float32 [3, 16, 128, 2048], P(None, 'dev', 'gx', 'gy')
The draws below stay inside these ranges and needn't reach their ends.
All inputs are finite; a program needn't handle non-finite values.
Results may differ from the reference program's by a relative error of at most 0.0001.
Values sent between devices are 32-bit elements; how exact they have to be, the bound alone decides.
A program may use at most 64 MiB of HBM per device.

```python
import math
import jax
import jax.numpy as jnp

STEPS = 2
NXF = 256
NYF = 4096
FZ = 8
NXC = 128
NYC = 2048
CZ = 16


def shard_levels(own_key, dims, cuts, smallest, top_value):
    def one(position, parts):
        steps = jax.random.uniform(jax.random.fold_in(jax.random.fold_in(own_key, 6), position), (parts,), jnp.float32, smallest / len(cuts), top_value / len(cuts))
        return jnp.repeat(jnp.exp(steps), dims[position] // parts).reshape((-1,) + (1,) * (len(dims) - position - 1))

    factor_of = one(*cuts[0])
    for cut in cuts[1:]:
        factor_of = factor_of * one(*cut)
    return factor_of


def normal_values(stream_key, extent, deviation, reach, pieces=(), kind=jnp.bfloat16):
    gain = shard_levels(stream_key, extent, pieces, -0.22, 0.18) if pieces else 1.0
    array = jax.random.normal(stream_key, extent, jnp.float32) * deviation * gain
    return jnp.minimum(jnp.maximum(array, -reach), reach).astype(kind)


def setup_inputs(seed: int = 0) -> dict:
    key_list = jax.random.split(jax.random.key(seed), 7)
    return {
        "fine_now": normal_values(key_list[0], (3, FZ, NXF, NYF), 1.0, 6.0, ((1, 2), (2, 16), (3, 16)), jnp.float32),
        "fine_before": normal_values(key_list[1], (3, FZ, NXF, NYF), 1.0, 6.0, ((1, 2), (2, 16), (3, 16)), jnp.float32),
        "fine_material": jnp.clip(jnp.exp(math.log(2.0) - 1.3862944 * jax.random.uniform(key_list[2], (4, FZ, NXF, NYF), jnp.float32) ** shard_levels(key_list[2], (4, FZ, NXF, NYF), ((1, 2), (2, 16), (3, 16)), -0.2, 0.2)), 0.5, 2.0),
        "coarse_now": normal_values(key_list[3], (3, CZ, NXC, NYC), 1.0, 6.0, ((1, 2), (2, 16), (3, 16)), jnp.float32),
        "coarse_before": normal_values(key_list[4], (3, CZ, NXC, NYC), 1.0, 6.0, ((1, 2), (2, 16), (3, 16)), jnp.float32),
        "coarse_material": jnp.clip(jnp.exp(math.log(2.0) - 1.3862944 * jax.random.uniform(key_list[5], (3, CZ, NXC, NYC), jnp.float32) ** shard_levels(key_list[5], (3, CZ, NXC, NYC), ((1, 2), (2, 16), (3, 16)), -0.2, 0.2)), 0.5, 2.0),
    }


time_step = 0.15


def restrict(plane):
    return plane.reshape(plane.shape[0], plane.shape[1] // 2, 2, plane.shape[2] // 2, 2).mean(axis=(2, 4))


def prolong(plane):
    return jnp.repeat(jnp.repeat(plane, 2, axis=1), 2, axis=2)


def backward(field, direction):
    inner = field[1:, 1:, 1:]
    if direction == 0:
        return inner - field[:-1, 1:, 1:]
    if direction == 1:
        return inner - field[1:, :-1, 1:]
    return inner - field[1:, 1:, :-1]


def forces(padded, medium, spacing, stretched):
    centre = padded[:, :-1, :-1, :-1]
    medium_cells = medium[:, :, :-1, :-1]
    if stretched:
        vertical = medium_cells[3] / spacing
        outward = medium[3, 1:, 1:-1, 1:-1] / spacing
    else:
        vertical = 1.0 / spacing
        outward = 1.0 / spacing
    along_z = (padded[:, 1:, :-1, :-1] - centre) * vertical
    along_x = (padded[:, :-1, 1:, :-1] - centre) / spacing
    along_y = (padded[:, :-1, :-1, 1:] - centre) / spacing
    rigidity = medium_cells[1]
    lame_first = medium_cells[2]
    dilation = along_x[0] + along_y[1] + along_z[2]
    normal_x = lame_first * dilation + 2.0 * rigidity * along_x[0]
    normal_y = lame_first * dilation + 2.0 * rigidity * along_y[1]
    normal_z = lame_first * dilation + 2.0 * rigidity * along_z[2]
    shear_xy = rigidity * (along_y[0] + along_x[1])
    shear_xz = rigidity * (along_z[0] + along_x[2])
    shear_yz = rigidity * (along_z[1] + along_y[2])
    force_x = (backward(normal_x, 1) + backward(shear_xy, 2)) / spacing + backward(shear_xz, 0) * outward
    force_y = (backward(shear_xy, 1) + backward(normal_y, 2)) / spacing + backward(shear_yz, 0) * outward
    force_z = (backward(shear_xz, 1) + backward(shear_yz, 2)) / spacing + backward(normal_z, 0) * outward
    return jnp.stack([force_x, force_y, force_z])


def advance(field, before, padded, medium, density, spacing, stretched):
    return 2.0 * field - before + (time_step * time_step) * forces(padded, medium, spacing, stretched) / density


def pad_sides(field):
    return jnp.pad(field, ((0, 0), (0, 0), (1, 1), (1, 1)))


def reference(fine_now, fine_before, fine_material, coarse_now, coarse_before, coarse_material):
    fine_medium = pad_sides(jnp.concatenate([jnp.zeros_like(fine_material[:, :1]), fine_material], axis=1))
    coarse_medium = pad_sides(jnp.concatenate([coarse_material[:, :1], coarse_material], axis=1))
    for instant in range(STEPS):
        fine_ghost = prolong(coarse_now[:, 0])
        coarse_ghost = restrict(fine_now[:, -1])
        fine_padded = pad_sides(jnp.concatenate([jnp.zeros_like(fine_now[:, :1]), fine_now, fine_ghost[:, None]], axis=1))
        coarse_padded = pad_sides(jnp.concatenate([coarse_ghost[:, None], coarse_now, jnp.zeros_like(coarse_now[:, :1])], axis=1))
        fine_next = advance(fine_now, fine_before, fine_padded, fine_medium, fine_material[0], 1.0, True)
        coarse_next = advance(coarse_now, coarse_before, coarse_padded, coarse_medium, coarse_material[0], 2.0, False)
        fine_before, fine_now = fine_now, fine_next
        coarse_before, coarse_now = coarse_now, coarse_next
    return fine_now, coarse_now
```

```python
import jax
import jax.numpy as jnp
from jax import lax
from jax.experimental import pallas as pl
from jax.experimental.pallas import tpu as pltpu
from jax.sharding import PartitionSpec as P

STEPS = 2
STEP_SQUARED = 0.15 * 0.15
MESH = pl.DeviceIdType.MESH
F32 = jnp.float32
BF16 = jnp.bfloat16

FR, FW = 24, 384
CR, CW = 16, 256
FL, CL = 4, 8
FQ = 10
CQ = 9

X_FINE = FQ * 16
X_COARSE = 14 * 8
X_EXTRA = 3 * 16
X_ROWS = X_FINE + X_COARSE + X_EXTRA
X_LOW_ROWS = X_FINE + X_COARSE
Y_FINE = 32
Y_COARSE = 24
C_FINE = 16
Y_ROWS = Y_FINE + Y_COARSE
C_ROWS = Y_COARSE + C_FINE
SIDES = ((-1, 0), (1, 0), (0, -1), (0, 1), (-1, -1), (-1, 1), (1, -1), (1, 1))


def iota(shape, dim):
    return lax.broadcasted_iota(jnp.int32, shape, dim)


def turned(value, shift, axis):
    shift = shift % value.shape[axis]
    return pltpu.roll(value, shift, axis) if shift else value


def parts(value):
    high = value.astype(BF16)
    rest = value - high.astype(F32)
    middle = rest.astype(BF16)
    return high, middle, (rest - middle.astype(F32)).astype(BF16)


def times_right(value, matrix):
    return sum(jnp.dot(part, matrix, preferred_element_type=F32) for part in parts(value))


def times_left(matrix, value):
    return sum(jnp.dot(matrix, part, preferred_element_type=F32) for part in parts(value))


def coarse_place(fine, half):
    halo = jnp.where(fine < half, fine // 2, fine // 2 + half)
    return jnp.where(fine < 2 * half, halo, fine // 2 + half)


def gradients_to_stress(here, below, medium, stretch, which):
    def ahead(value, axis):
        return turned(value, -1, axis)

    mu, lam = medium
    dz = [b - h for b, h in zip(below, here)]
    if stretch is not None:
        dz = [d * stretch for d in dz]
    dx = [ahead(h, 0) - h for h in here]
    dy = [ahead(h, 1) - h for h in here]
    bulk = lam * (dx[0] + dy[1] + dz[2])
    twice = mu + mu
    out = {"zz": bulk + twice * dz[2], "xz": mu * (dz[0] + dx[2]), "yz": mu * (dz[1] + dy[2])}
    if which == "all":
        out["xx"] = bulk + twice * dx[0]
        out["yy"] = bulk + twice * dy[1]
        out["xy"] = mu * (dy[0] + dx[1])
    return out


def step(count, cur, qty, before_at, scale_at, stretched, zs, write, crop):
    r0, w0 = crop

    def stress(slot, which):
        medium = (qty[3, slot], qty[4, slot])
        stretch = qty[5, slot] if stretched else None
        return gradients_to_stress(
            [cur[c, slot] for c in range(3)], [cur[c, slot + 1] for c in range(3)], medium, stretch, which
        )

    def cut(value):
        return value[r0:, w0:]

    top = stress(0, "vertical")
    for k, name in enumerate(("xz", "yz", "zz")):
        zs[k] = top[name]

    def body(slot, carry):
        s = stress(slot, "all")

        def back_x(name):
            return cut(s[name]) - cut(turned(s[name], 1, 0))

        def back_y(name):
            return cut(s[name]) - cut(turned(s[name], 1, 1))

        def back_z(k, name):
            d = cut(s[name]) - cut(zs[k])
            return d * cut(qty[5, slot]) if stretched else d

        force = (
            back_x("xx") + back_y("xy") + back_z(0, "xz"),
            back_x("xy") + back_y("yy") + back_z(1, "yz"),
            back_x("xz") + back_y("yz") + back_z(2, "zz"),
        )
        scale = cut(qty[scale_at, slot])
        for c in range(3):
            now = cut(cur[c, slot])
            write(c, slot, now + now - before_at(c, slot)[r0:, w0:] + scale * force[c])
        for k, name in enumerate(("xz", "yz", "zz")):
            zs[k] = s[name]
        return carry

    lax.fori_loop(1, count + 1, body, 0)


def pack_x(qf, qc, low, high):
    row8 = iota((8, 256), 0)
    crow = iota((8, 128), 0)

    def store(ref, at, value):
        ref[pl.ds(at, 8), :] = value[:, :128]
        ref[pl.ds(at + 8, 8), :] = value[:, 128:]

    for g in range(FQ):
        up = jnp.zeros((8, 256), F32)
        down = up
        for l in range(FL):
            z = jnp.where(row8 < 4, qf[g, l + 1, 8:16, 128:], qf[g, l + 1, 16:24, 128:])
            t = turned(z, 2 * l, 0)
            up = t if l == 0 else jnp.where(row8 // 2 == l, t, up)
            down = t if l == 0 else jnp.where(row8 // 2 == l - 1, t, down)
        store(high, g * 16, up)
        store(low, g * 16, down)
    for q in range(5):
        for half in range(2):
            for l in range(4):
                t = turned(qc[q, half * 4 + l + 1, 8:16, 128:], 2 * l, 0)
                up = t if l == 0 else jnp.where(crow // 2 == l, t, up)
                down = t if l == 0 else jnp.where(crow // 2 == l - 1, t, down)
            at = X_FINE + (q * 2 + half) * 8
            high[pl.ds(at, 8), :] = up
            low[pl.ds(at, 8), :] = down
    for q in range(4):
        for l in range(8):
            t = turned(qc[5 + q, l + 1, 8:16, 128:], l, 0)
            up = t if l == 0 else jnp.where(crow == l, t, up)
            down = t if l == 0 else jnp.where(crow == l - 1, t, down)
        at = X_FINE + (10 + q) * 8
        high[pl.ds(at, 8), :] = up
        low[pl.ds(at, 8), :] = down
    for c in range(3):
        more = jnp.where(row8 < 2, turned(qf[c, 3, 8:16, 128:], -2, 0), qf[c, 4, 8:16, 128:])
        store(high, X_FINE + X_COARSE + c * 16, more)


def unpack_x(qf, qc, low, high):
    row8 = iota((8, 256), 0)
    crow = iota((8, 128), 0)

    def load(ref, at):
        return jnp.concatenate([ref[pl.ds(at, 8), :], ref[pl.ds(at + 8, 8), :]], axis=1)

    for g in range(FQ):
        up = load(high, g * 16)
        down = load(low, g * 16)
        more = load(high, X_FINE + X_COARSE + g * 16) if g < 3 else None
        for l in range(FL):
            t = jnp.where(row8 < 4, turned(up, -2 * l, 0), turned(down, -2 * l, 0))
            if g < 3 and l == 2:
                t = jnp.where(row8 // 2 == 1, turned(more, 2, 0), t)
            if g < 3 and l == 3:
                t = jnp.where(row8 // 2 == 1, more, t)
            qf[g, l + 1, 0:8, 128:] = t
    for q in range(5):
        for half in range(2):
            at = X_FINE + (q * 2 + half) * 8
            up = high[pl.ds(at, 8), :]
            down = low[pl.ds(at, 8), :]
            for l in range(4):
                t = jnp.where(crow < 4, turned(up, -2 * l, 0), turned(down, -2 * l, 0))
                qc[q, half * 4 + l + 1, 0:8, 128:] = t
    for q in range(4):
        at = X_FINE + (10 + q) * 8
        up = high[pl.ds(at, 8), :]
        down = low[pl.ds(at, 8), :]
        for l in range(8):
            qc[5 + q, l + 1, 0:8, 128:] = jnp.where(crow < 4, turned(up, -l, 0), turned(down, -l, 0))


def pack_y(qf, qc, out):
    lane = iota((16, 128), 1)
    lane8 = iota((8, 128), 1)
    row8 = iota((8, 128), 0)
    for t in range(2):
        packed = jnp.zeros((16, 128), F32)
        for k in range(20):
            g, l = t * 5 + k // 4, k % 4
            z = jnp.where(lane < 64, qf[g, l + 1, 8:24, 128:256], qf[g, l + 1, 8:24, 256:384])
            mine = ((lane + (2 - 6 * k + 128)) & 127) < 6
            packed = jnp.where(mine, turned(z, 6 * k, 1), packed)
        out[pl.ds(t * 16, 16), :] = packed
        out[pl.ds(Y_ROWS + t * 8, 8), :] = jnp.where(row8 < 4, packed[:8], packed[8:])
    for t in range(3):
        packed = jnp.zeros((8, 128), F32)
        for k in range(32 if t < 2 else 8):
            q, l = t * 4 + k // 8, k % 8
            mine = ((lane8 + (2 - 4 * k + 128)) & 127) < 4
            packed = jnp.where(mine, turned(qc[q, l + 1, 8:16, 128:256], 4 * k, 1), packed)
        out[pl.ds(Y_FINE + t * 8, 8), :] = packed


def unpack_y(qf, qc, side, corner):
    lane = iota((16, 128), 1)
    lane8 = iota((8, 128), 1)
    row8 = iota((8, 128), 0)
    fine_low = ((lane + 2) & 127) % 6 < 2
    fine_low8 = ((lane8 + 2) & 127) % 6 < 2
    coarse_low8 = ((lane8 + 2) & 127) % 4 < 2

    def corners(at, low):
        before = jnp.where(low, corner[0, pl.ds(at, 8), :], corner[1, pl.ds(at, 8), :])
        after = jnp.where(low, corner[2, pl.ds(at, 8), :], corner[3, pl.ds(at, 8), :])
        return jnp.where(row8 < 4, after, before)

    for t in range(2):
        own = jnp.where(fine_low, side[0, pl.ds(t * 16, 16), :], side[1, pl.ds(t * 16, 16), :])
        both = jnp.concatenate([corners(Y_COARSE + t * 8, fine_low8), own], axis=0)
        for k in range(20):
            g, l = t * 5 + k // 4, k % 4
            qf[g, l + 1, :, 0:128] = turned(both, -6 * k, 1)
    for t in range(3):
        at = Y_FINE + t * 8
        own = jnp.where(coarse_low8, side[0, pl.ds(at, 8), :], side[1, pl.ds(at, 8), :])
        both = jnp.concatenate([corners(t * 8, coarse_low8), own], axis=0)
        for k in range(32 if t < 2 else 8):
            q, l = t * 4 + k // 8, k % 8
            qc[q, l + 1, :, 0:128] = turned(both, -4 * k, 1)


def kernel(
    fine_now, fine_before, fine_material, coarse_now, coarse_before, coarse_material,
    fine_out, coarse_out,
    qf, qc, u1f, u1c, zf, zc,
    sx_low, sx_high, sy, rx_low, rx_high, ry, rc,
    give, got, lanes_down, lanes_up, rows_down, rows_up,
    load_sem, send_sem, recv_sem, deep_send, deep_recv,
):
    gx, gy, dev = lax.axis_index("gx"), lax.axis_index("gy"), lax.axis_index("dev")
    nx, ny = lax.axis_size("gx"), lax.axis_size("gy")
    top = dev == 0
    partner = {"gx": gx, "gy": gy, "dev": 1 - dev}
    there = []
    for dx, dy in SIDES:
        x, y = gx + dx, gy + dy
        there.append(({"gx": x, "gy": y, "dev": dev}, (x >= 0) & (x < nx) & (y >= 0) & (y < ny)))

    barrier = pltpu.get_barrier_semaphore()
    expected = 1
    pl.semaphore_signal(barrier, inc=1, device_id=partner, device_id_type=MESH)
    for where, present in there:
        @pl.when(present)
        def _(where=where):
            pl.semaphore_signal(barrier, inc=1, device_id=where, device_id_type=MESH)
        expected = expected + jnp.where(present, 1, 0)

    fine_own = (pl.ds(1, FL), pl.ds(8, 16), pl.ds(128, 256))
    coarse_own = (pl.ds(1, CL), pl.ds(8, 8), pl.ds(128, 128))
    loads = [
        (fine_now, qf.at[(pl.ds(0, 3), *fine_own)]),
        (fine_material.at[pl.ds(1, 3)], qf.at[(pl.ds(3, 3), *fine_own)]),
        (fine_before, qf.at[(pl.ds(6, 3), *fine_own)]),
        (fine_material.at[pl.ds(0, 1)], qf.at[(pl.ds(9, 1), *fine_own)]),
        (coarse_now, qc.at[(pl.ds(0, 3), *coarse_own)]),
        (coarse_material.at[pl.ds(1, 2)], qc.at[(pl.ds(3, 2), *coarse_own)]),
        (coarse_before, qc.at[(pl.ds(5, 3), *coarse_own)]),
        (coarse_material.at[pl.ds(0, 1)], qc.at[(pl.ds(8, 1), *coarse_own)]),
    ]
    copies = [pltpu.make_async_copy(src, dst, load_sem.at[k]) for k, (src, dst) in enumerate(loads)]
    for copy in copies:
        copy.start()

    def zero_unless(present, ref, at=None):
        @pl.when(jnp.logical_not(present))
        def _():
            if at is None:
                ref[...] = jnp.zeros(ref.shape, F32)
            else:
                ref[at] = jnp.zeros(ref.shape[1:], F32)

    zero_unless(there[0][1], rx_low)
    zero_unless(there[1][1], rx_high)
    for k in range(2):
        zero_unless(there[2 + k][1], ry, k)
    for k in range(4):
        zero_unless(there[4 + k][1], rc, k)

    @pl.when(top)
    def _():
        for c in range(3):
            qf[c, 0] = jnp.zeros((FR, FW), F32)
            u1f[c, 0] = jnp.zeros((FR, FW), F32)
        for k in range(3, 6):
            qf[k, 0] = jnp.zeros((FR, FW), F32)

    @pl.when(jnp.logical_not(top))
    def _():
        for c in range(3):
            qc[c, CL + 1] = jnp.zeros((CR, CW), F32)
            u1c[c, CL + 1] = jnp.zeros((CR, CW), F32)
        place = coarse_place(iota((FW, CW), 0), 64)
        lanes_down[...] = jnp.where(place == iota((FW, CW), 1), 0.5, 0.0).astype(BF16)
        place = coarse_place(iota((CW, FW), 1), 64)
        lanes_up[...] = jnp.where(place == iota((CW, FW), 0), 1.0, 0.0).astype(BF16)

        def rows(shape, fine_dim):
            fine, coarse = iota(shape, fine_dim), iota(shape, 1 - fine_dim)
            place = coarse_place(fine % FR, 4)
            return (place == coarse % CR) & (fine // FR == coarse // CR)

        rows_down[...] = jnp.where(rows((3 * CR, 3 * FR), 1), 0.5, 0.0).astype(BF16)
        rows_up[...] = jnp.where(rows((3 * FR, 3 * CR), 0), 1.0, 0.0).astype(BF16)

    for copy in copies:
        copy.wait()
    for l in range(FL):
        own = (9, l + 1, pl.ds(8, 16), pl.ds(128, 256))
        qf[own] = STEP_SQUARED / qf[own]
    for l in range(CL):
        own = (8, l + 1, pl.ds(8, 8), pl.ds(128, 128))
        qc[own] = (0.25 * STEP_SQUARED) / qc[own]
    pack_x(qf, qc, sx_low, sx_high)
    pack_y(qf, qc, sy)
    pl.semaphore_wait(barrier, expected)

    side_msg, corner_msg = sy.at[pl.ds(0, Y_ROWS)], sy.at[pl.ds(Y_FINE, C_ROWS)]
    messages = [
        (sx_high, rx_high), (sx_low, rx_low), (side_msg, ry.at[1]), (side_msg, ry.at[0]),
        (corner_msg, rc.at[3]), (corner_msg, rc.at[2]), (corner_msg, rc.at[1]), (corner_msg, rc.at[0]),
    ]
    sends = []
    for k, (src, dst) in enumerate(messages):
        copy = pltpu.make_async_remote_copy(
            src, dst, send_sem.at[k], recv_sem.at[k], device_id=there[k][0], device_id_type=MESH
        )

        @pl.when(there[k][1])
        def _(copy=copy):
            copy.start()

        sends.append(copy)

    def arrived(k):
        opposite = SIDES.index((-SIDES[k][0], -SIDES[k][1]))

        @pl.when(there[opposite][1])
        def _():
            sends[k].wait_recv()

    for k in range(8):
        arrived(k)
    unpack_x(qf, qc, rx_low, rx_high)
    unpack_y(qf, qc, ry, rc)

    def deep_exchange(phase, cur_f, cur_c):
        mine_f, theirs_f = jnp.where(top, FL, 1), jnp.where(top, 0, FL + 1)
        mine_c, theirs_c = jnp.where(top, CL, 1), jnp.where(top, 0, CL + 1)

        @pl.when(top)
        def _():
            for c in range(3):
                give[phase, c] = cur_c[c, 1]

        @pl.when(jnp.logical_not(top))
        def _():
            fine = jnp.concatenate([cur_f[c, FL] for c in range(3)], axis=0)
            small = times_left(rows_down[...], times_right(fine, lanes_down[...]))
            for c in range(3):
                give[phase, c] = small[c * CR : (c + 1) * CR]

        moves = [
            (cur_f.at[pl.ds(0, 3), mine_f], cur_f.at[pl.ds(0, 3), theirs_f]),
            (cur_c.at[pl.ds(0, 3), mine_c], cur_c.at[pl.ds(0, 3), theirs_c]),
            (give.at[phase], got.at[phase]),
        ]
        copies = [
            pltpu.make_async_remote_copy(
                src, dst, deep_send.at[phase, k], deep_recv.at[phase, k], device_id=partner, device_id_type=MESH
            )
            for k, (src, dst) in enumerate(moves)
        ]
        for copy in copies:
            copy.start()
        if phase == 0:
            medium = [
                pltpu.make_async_remote_copy(
                    src, dst, deep_send.at[0, 3 + k], deep_recv.at[0, 3 + k], device_id=partner, device_id_type=MESH
                )
                for k, (src, dst) in enumerate(
                    (
                        (qf.at[pl.ds(3, 3), FL], qf.at[pl.ds(3, 3), 0]),
                        (qc.at[pl.ds(3, 2), CL], qc.at[pl.ds(3, 2), 0]),
                    )
                )
            ]

            @pl.when(top)
            def _():
                for copy in medium:
                    copy.start()
                for k in range(3, 5):
                    qc[k, 0] = qc[k, 1]
        for copy in copies:
            copy.wait_recv()

        @pl.when(top)
        def _():
            for c in range(3):
                cur_c[c, 0] = got[phase, c]

        @pl.when(jnp.logical_not(top))
        def _():
            coarse = jnp.concatenate([got[phase, c] for c in range(3)], axis=0)
            large = times_left(rows_up[...], times_right(coarse, lanes_up[...]))
            for c in range(3):
                cur_f[c, FL + 1] = large[c * FR : (c + 1) * FR]

        for copy in copies:
            copy.wait_send()
        if phase == 0:
            @pl.when(top)
            def _():
                for copy in medium:
                    copy.wait_send()

            @pl.when(jnp.logical_not(top))
            def _():
                for copy in medium:
                    copy.wait_recv()

    deep_exchange(0, qf, qc)

    def keep_f(c, slot, value):
        u1f[c, slot] = value

    def keep_c(c, slot, value):
        u1c[c, slot] = value

    step(FL, qf, qf, lambda c, s: qf[6 + c, s], 9, True, zf, keep_f, (0, 0))
    step(CL, qc, qc, lambda c, s: qc[5 + c, s], 8, False, zc, keep_c, (0, 0))

    deep_exchange(1, u1f, u1c)

    def out_f(c, slot, value):
        fine_out[c, slot - 1] = value

    def out_c(c, slot, value):
        coarse_out[c, slot - 1] = value

    step(FL, u1f, qf, lambda c, s: qf[c, s], 9, True, zf, out_f, (8, 128))
    step(CL, u1c, qc, lambda c, s: qc[c, s], 8, False, zc, out_c, (8, 128))

    for k, copy in enumerate(sends):
        @pl.when(there[k][1])
        def _(copy=copy):
            copy.wait_send()


def per_device(*arrays):
    fine, coarse = arrays[0], arrays[3]
    return pl.pallas_call(
        kernel,
        out_shape=(jax.ShapeDtypeStruct(fine.shape, F32), jax.ShapeDtypeStruct(coarse.shape, F32)),
        in_specs=[pl.BlockSpec(memory_space=pltpu.HBM)] * 6,
        out_specs=(pl.BlockSpec(memory_space=pltpu.VMEM), pl.BlockSpec(memory_space=pltpu.VMEM)),
        scratch_shapes=[
            pltpu.VMEM((FQ, FL + 2, FR, FW), F32),
            pltpu.VMEM((CQ, CL + 2, CR, CW), F32),
            pltpu.VMEM((3, FL + 2, FR, FW), F32),
            pltpu.VMEM((3, CL + 2, CR, CW), F32),
            pltpu.VMEM((3, FR, FW), F32),
            pltpu.VMEM((3, CR, CW), F32),
            pltpu.VMEM((X_LOW_ROWS, 128), F32),
            pltpu.VMEM((X_ROWS, 128), F32),
            pltpu.VMEM((Y_ROWS + C_FINE, 128), F32),
            pltpu.VMEM((X_LOW_ROWS, 128), F32),
            pltpu.VMEM((X_ROWS, 128), F32),
            pltpu.VMEM((2, Y_ROWS, 128), F32),
            pltpu.VMEM((4, C_ROWS, 128), F32),
            pltpu.VMEM((STEPS, 3, CR, CW), F32),
            pltpu.VMEM((STEPS, 3, CR, CW), F32),
            pltpu.VMEM((FW, CW), BF16),
            pltpu.VMEM((CW, FW), BF16),
            pltpu.VMEM((3 * CR, 3 * FR), BF16),
            pltpu.VMEM((3 * FR, 3 * CR), BF16),
            pltpu.SemaphoreType.DMA((8,)),
            pltpu.SemaphoreType.DMA((8,)),
            pltpu.SemaphoreType.DMA((8,)),
            pltpu.SemaphoreType.DMA((STEPS, 5)),
            pltpu.SemaphoreType.DMA((STEPS, 5)),
        ],
        compiler_params=pltpu.CompilerParams(
            collective_id=0, has_side_effects=True, vmem_limit_bytes=40 * 2**20
        ),
    )(*arrays)


def solution(mesh):
    spec = P(None, "dev", "gx", "gy")
    return jax.shard_map(
        per_device, mesh=mesh, in_specs=(spec,) * 6, out_specs=(spec, spec), check_vma=False
    )
```

```python
import jax
import jax.numpy as jnp
from jax import lax
from jax.experimental import pallas as pl
from jax.experimental.pallas import tpu as pltpu
from jax.sharding import PartitionSpec as P

STEPS = 2
STEP_SQUARED = 0.15 * 0.15
MESH = pl.DeviceIdType.MESH
F32 = jnp.float32
BF16 = jnp.bfloat16

FR, FW = 24, 384
CR, CW = 16, 256
FL, CL = 4, 8
FQ = 10
CQ = 9

X_FINE = FQ * 16
X_COARSE = 14 * 8
X_EXTRA = 3 * 16
X_ROWS = X_FINE + X_COARSE + X_EXTRA
X_LOW_ROWS = X_FINE + X_COARSE
Y_FINE = 32
Y_COARSE = 24
C_FINE = 16
Y_ROWS = Y_FINE + Y_COARSE
C_ROWS = Y_COARSE + C_FINE
SIDES = ((-1, 0), (1, 0), (0, -1), (0, 1), (-1, -1), (-1, 1), (1, -1), (1, 1))


def iota(shape, dim):
    return lax.broadcasted_iota(jnp.int32, shape, dim)


def turned(value, shift, axis):
    shift = shift % value.shape[axis]
    return pltpu.roll(value, shift, axis) if shift else value


def parts(value):
    high = value.astype(BF16)
    rest = value - high.astype(F32)
    middle = rest.astype(BF16)
    return high, middle, (rest - middle.astype(F32)).astype(BF16)


def times_right(value, matrix):
    return sum(jnp.dot(part, matrix, preferred_element_type=F32) for part in parts(value))


def times_left(matrix, value):
    return sum(jnp.dot(matrix, part, preferred_element_type=F32) for part in parts(value))


def coarse_place(fine, half):
    halo = jnp.where(fine < half, fine // 2, fine // 2 + half)
    return jnp.where(fine < 2 * half, halo, fine // 2 + half)


def gradients_to_stress(here, below, medium, stretch, which):
    def ahead(value, axis):
        return turned(value, -1, axis)

    mu, lam = medium
    dz = [b - h for b, h in zip(below, here)]
    if stretch is not None:
        dz = [d * stretch for d in dz]
    dx = [ahead(h, 0) - h for h in here]
    dy = [ahead(h, 1) - h for h in here]
    bulk = lam * (dx[0] + dy[1] + dz[2])
    twice = mu + mu
    out = {"zz": bulk + twice * dz[2], "xz": mu * (dz[0] + dx[2]), "yz": mu * (dz[1] + dy[2])}
    if which == "all":
        out["xx"] = bulk + twice * dx[0]
        out["yy"] = bulk + twice * dy[1]
        out["xy"] = mu * (dy[0] + dx[1])
    return out


class Step:
    def __init__(self, count, cur, qty, before_at, scale_at, stretched, write, crop):
        self.count, self.cur, self.qty, self.before_at = count, cur, qty, before_at
        self.scale_at, self.stretched, self.write, self.crop = scale_at, stretched, write, crop

    def cut(self, value):
        return value[self.crop[0] :, self.crop[1] :]

    def stress(self, slot, which="all"):
        cur, qty = self.cur, self.qty
        stretch = qty[5, slot] if self.stretched else None
        return gradients_to_stress(
            [cur[c, slot] for c in range(3)],
            [cur[c, slot + 1] for c in range(3)],
            (qty[3, slot], qty[4, slot]),
            stretch,
            which,
        )

    def move(self, slot, s, above):
        cut = self.cut

        def back_x(name):
            return cut(s[name]) - cut(turned(s[name], 1, 0))

        def back_y(name):
            return cut(s[name]) - cut(turned(s[name], 1, 1))

        def back_z(name):
            d = cut(s[name]) - cut(above[name])
            return d * cut(self.qty[5, slot]) if self.stretched else d

        force = (
            back_x("xx") + back_y("xy") + back_z("xz"),
            back_x("xy") + back_y("yy") + back_z("yz"),
            back_x("xz") + back_y("yz") + back_z("zz"),
        )
        scale = cut(self.qty[self.scale_at, slot])
        for c in range(3):
            now = cut(self.cur[c, slot])
            before = cut(self.before_at(c, slot))
            self.write(c, slot, now + now - before + scale * force[c])

    def inner(self):
        self.first = above = self.stress(1)
        for slot in range(2, self.count):
            s = self.stress(slot)
            self.move(slot, s, above)
            above = s
        self.above = above

    def outer(self):
        last = self.stress(self.count)
        self.move(self.count, last, self.above)
        self.move(1, self.first, self.stress(0, "vertical"))


def pack_x(qf, qc, low, high):
    row8 = iota((8, 256), 0)
    crow = iota((8, 128), 0)

    def store(ref, at, value):
        ref[pl.ds(at, 8), :] = value[:, :128]
        ref[pl.ds(at + 8, 8), :] = value[:, 128:]

    for g in range(FQ):
        up = jnp.zeros((8, 256), F32)
        down = up
        for l in range(FL):
            z = jnp.where(row8 < 4, qf[g, l + 1, 8:16, 128:], qf[g, l + 1, 16:24, 128:])
            t = turned(z, 2 * l, 0)
            up = t if l == 0 else jnp.where(row8 // 2 == l, t, up)
            down = t if l == 0 else jnp.where(row8 // 2 == l - 1, t, down)
        store(high, g * 16, up)
        store(low, g * 16, down)
    for q in range(5):
        for half in range(2):
            for l in range(4):
                t = turned(qc[q, half * 4 + l + 1, 8:16, 128:], 2 * l, 0)
                up = t if l == 0 else jnp.where(crow // 2 == l, t, up)
                down = t if l == 0 else jnp.where(crow // 2 == l - 1, t, down)
            at = X_FINE + (q * 2 + half) * 8
            high[pl.ds(at, 8), :] = up
            low[pl.ds(at, 8), :] = down
    for q in range(4):
        for l in range(8):
            t = turned(qc[5 + q, l + 1, 8:16, 128:], l, 0)
            up = t if l == 0 else jnp.where(crow == l, t, up)
            down = t if l == 0 else jnp.where(crow == l - 1, t, down)
        at = X_FINE + (10 + q) * 8
        high[pl.ds(at, 8), :] = up
        low[pl.ds(at, 8), :] = down
    for c in range(3):
        more = jnp.where(row8 < 2, turned(qf[c, 3, 8:16, 128:], -2, 0), qf[c, 4, 8:16, 128:])
        store(high, X_FINE + X_COARSE + c * 16, more)


def unpack_x(qf, qc, low, high):
    row8 = iota((8, 256), 0)
    crow = iota((8, 128), 0)

    def load(ref, at):
        return jnp.concatenate([ref[pl.ds(at, 8), :], ref[pl.ds(at + 8, 8), :]], axis=1)

    for g in range(FQ):
        up = load(high, g * 16)
        down = load(low, g * 16)
        more = load(high, X_FINE + X_COARSE + g * 16) if g < 3 else None
        for l in range(FL):
            t = jnp.where(row8 < 4, turned(up, -2 * l, 0), turned(down, -2 * l, 0))
            if g < 3 and l == 2:
                t = jnp.where(row8 // 2 == 1, turned(more, 2, 0), t)
            if g < 3 and l == 3:
                t = jnp.where(row8 // 2 == 1, more, t)
            qf[g, l + 1, 0:8, 128:] = t
    for q in range(5):
        for half in range(2):
            at = X_FINE + (q * 2 + half) * 8
            up = high[pl.ds(at, 8), :]
            down = low[pl.ds(at, 8), :]
            for l in range(4):
                t = jnp.where(crow < 4, turned(up, -2 * l, 0), turned(down, -2 * l, 0))
                qc[q, half * 4 + l + 1, 0:8, 128:] = t
    for q in range(4):
        at = X_FINE + (10 + q) * 8
        up = high[pl.ds(at, 8), :]
        down = low[pl.ds(at, 8), :]
        for l in range(8):
            qc[5 + q, l + 1, 0:8, 128:] = jnp.where(crow < 4, turned(up, -l, 0), turned(down, -l, 0))


def pack_y(qf, qc, out):
    lane = iota((16, 128), 1)
    lane8 = iota((8, 128), 1)
    row8 = iota((8, 128), 0)
    for t in range(2):
        packed = jnp.zeros((16, 128), F32)
        for k in range(20):
            g, l = t * 5 + k // 4, k % 4
            z = jnp.where(lane < 64, qf[g, l + 1, 8:24, 128:256], qf[g, l + 1, 8:24, 256:384])
            mine = ((lane + (2 - 6 * k + 128)) & 127) < 6
            packed = jnp.where(mine, turned(z, 6 * k, 1), packed)
        out[pl.ds(t * 16, 16), :] = packed
        out[pl.ds(Y_ROWS + t * 8, 8), :] = jnp.where(row8 < 4, packed[:8], packed[8:])
    for t in range(3):
        packed = jnp.zeros((8, 128), F32)
        for k in range(32 if t < 2 else 8):
            q, l = t * 4 + k // 8, k % 8
            mine = ((lane8 + (2 - 4 * k + 128)) & 127) < 4
            packed = jnp.where(mine, turned(qc[q, l + 1, 8:16, 128:256], 4 * k, 1), packed)
        out[pl.ds(Y_FINE + t * 8, 8), :] = packed


def unpack_y(qf, qc, side, corner):
    lane = iota((16, 128), 1)
    lane8 = iota((8, 128), 1)
    row8 = iota((8, 128), 0)
    fine_low = ((lane + 2) & 127) % 6 < 2
    fine_low8 = ((lane8 + 2) & 127) % 6 < 2
    coarse_low8 = ((lane8 + 2) & 127) % 4 < 2

    def corners(at, low):
        before = jnp.where(low, corner[0, pl.ds(at, 8), :], corner[1, pl.ds(at, 8), :])
        after = jnp.where(low, corner[2, pl.ds(at, 8), :], corner[3, pl.ds(at, 8), :])
        return jnp.where(row8 < 4, after, before)

    for t in range(2):
        own = jnp.where(fine_low, side[0, pl.ds(t * 16, 16), :], side[1, pl.ds(t * 16, 16), :])
        both = jnp.concatenate([corners(Y_COARSE + t * 8, fine_low8), own], axis=0)
        for k in range(20):
            g, l = t * 5 + k // 4, k % 4
            qf[g, l + 1, :, 0:128] = turned(both, -6 * k, 1)
    for t in range(3):
        at = Y_FINE + t * 8
        own = jnp.where(coarse_low8, side[0, pl.ds(at, 8), :], side[1, pl.ds(at, 8), :])
        both = jnp.concatenate([corners(t * 8, coarse_low8), own], axis=0)
        for k in range(32 if t < 2 else 8):
            q, l = t * 4 + k // 8, k % 8
            qc[q, l + 1, :, 0:128] = turned(both, -4 * k, 1)


def kernel(
    fine_now, fine_before, fine_material, coarse_now, coarse_before, coarse_material,
    fine_out, coarse_out,
    qf, qc, u1f, u1c,
    sx_low, sx_high, sy, rx_low, rx_high, ry, rc,
    give, got, lanes_down, lanes_up, rows_down, rows_up,
    load_sem, send_sem, recv_sem, deep_send, deep_recv,
):
    gx, gy, dev = lax.axis_index("gx"), lax.axis_index("gy"), lax.axis_index("dev")
    nx, ny = lax.axis_size("gx"), lax.axis_size("gy")
    top = dev == 0
    partner = {"gx": gx, "gy": gy, "dev": 1 - dev}
    there = []
    for dx, dy in SIDES:
        x, y = gx + dx, gy + dy
        there.append(({"gx": x, "gy": y, "dev": dev}, (x >= 0) & (x < nx) & (y >= 0) & (y < ny)))

    barrier = pltpu.get_barrier_semaphore()
    expected = 1
    pl.semaphore_signal(barrier, inc=1, device_id=partner, device_id_type=MESH)
    for where, present in there:
        @pl.when(present)
        def _(where=where):
            pl.semaphore_signal(barrier, inc=1, device_id=where, device_id_type=MESH)
        expected = expected + jnp.where(present, 1, 0)

    fine_own = (pl.ds(1, FL), pl.ds(8, 16), pl.ds(128, 256))
    coarse_own = (pl.ds(1, CL), pl.ds(8, 8), pl.ds(128, 128))
    loads = [
        (fine_now, qf.at[(pl.ds(0, 3), *fine_own)]),
        (fine_material.at[pl.ds(1, 3)], qf.at[(pl.ds(3, 3), *fine_own)]),
        (fine_before, qf.at[(pl.ds(6, 3), *fine_own)]),
        (fine_material.at[pl.ds(0, 1)], qf.at[(pl.ds(9, 1), *fine_own)]),
        (coarse_now, qc.at[(pl.ds(0, 3), *coarse_own)]),
        (coarse_material.at[pl.ds(1, 2)], qc.at[(pl.ds(3, 2), *coarse_own)]),
        (coarse_before, qc.at[(pl.ds(5, 3), *coarse_own)]),
        (coarse_material.at[pl.ds(0, 1)], qc.at[(pl.ds(8, 1), *coarse_own)]),
    ]
    copies = [pltpu.make_async_copy(src, dst, load_sem.at[k]) for k, (src, dst) in enumerate(loads)]
    for copy in copies:
        copy.start()

    def zero_unless(present, ref, at=None):
        @pl.when(jnp.logical_not(present))
        def _():
            if at is None:
                ref[...] = jnp.zeros(ref.shape, F32)
            else:
                ref[at] = jnp.zeros(ref.shape[1:], F32)

    zero_unless(there[0][1], rx_low)
    zero_unless(there[1][1], rx_high)
    for k in range(2):
        zero_unless(there[2 + k][1], ry, k)
    for k in range(4):
        zero_unless(there[4 + k][1], rc, k)

    @pl.when(top)
    def _():
        for c in range(3):
            qf[c, 0] = jnp.zeros((FR, FW), F32)
            u1f[c, 0] = jnp.zeros((FR, FW), F32)
        for k in range(3, 6):
            qf[k, 0] = jnp.zeros((FR, FW), F32)

    @pl.when(jnp.logical_not(top))
    def _():
        for c in range(3):
            qc[c, CL + 1] = jnp.zeros((CR, CW), F32)
            u1c[c, CL + 1] = jnp.zeros((CR, CW), F32)
        place = coarse_place(iota((FW, CW), 0), 64)
        lanes_down[...] = jnp.where(place == iota((FW, CW), 1), 0.5, 0.0).astype(BF16)
        place = coarse_place(iota((CW, FW), 1), 64)
        lanes_up[...] = jnp.where(place == iota((CW, FW), 0), 1.0, 0.0).astype(BF16)

        def rows(shape, fine_dim):
            fine, coarse = iota(shape, fine_dim), iota(shape, 1 - fine_dim)
            place = coarse_place(fine % FR, 4)
            return (place == coarse % CR) & (fine // FR == coarse // CR)

        rows_down[...] = jnp.where(rows((3 * CR, 3 * FR), 1), 0.5, 0.0).astype(BF16)
        rows_up[...] = jnp.where(rows((3 * FR, 3 * CR), 0), 1.0, 0.0).astype(BF16)

    for copy in copies:
        copy.wait()
    for l in range(FL):
        own = (9, l + 1, pl.ds(8, 16), pl.ds(128, 256))
        qf[own] = STEP_SQUARED / qf[own]
    for l in range(CL):
        own = (8, l + 1, pl.ds(8, 8), pl.ds(128, 128))
        qc[own] = (0.25 * STEP_SQUARED) / qc[own]
    pack_x(qf, qc, sx_low, sx_high)
    pack_y(qf, qc, sy)
    pl.semaphore_wait(barrier, expected)

    side_msg, corner_msg = sy.at[pl.ds(0, Y_ROWS)], sy.at[pl.ds(Y_FINE, C_ROWS)]
    messages = [
        (sx_high, rx_high), (sx_low, rx_low), (side_msg, ry.at[1]), (side_msg, ry.at[0]),
        (corner_msg, rc.at[3]), (corner_msg, rc.at[2]), (corner_msg, rc.at[1]), (corner_msg, rc.at[0]),
    ]
    sends = []
    for k, (src, dst) in enumerate(messages):
        copy = pltpu.make_async_remote_copy(
            src, dst, send_sem.at[k], recv_sem.at[k], device_id=there[k][0], device_id_type=MESH
        )

        @pl.when(there[k][1])
        def _(copy=copy):
            copy.start()

        sends.append(copy)

    def arrived(k):
        opposite = SIDES.index((-SIDES[k][0], -SIDES[k][1]))

        @pl.when(there[opposite][1])
        def _():
            sends[k].wait_recv()

    for k in range(8):
        arrived(k)
    unpack_x(qf, qc, rx_low, rx_high)
    unpack_y(qf, qc, ry, rc)

    mine_f, theirs_f = jnp.where(top, FL, 1), jnp.where(top, 0, FL + 1)
    mine_c, theirs_c = jnp.where(top, CL, 1), jnp.where(top, 0, CL + 1)

    def deep_copy(src, dst, phase, k):
        return pltpu.make_async_remote_copy(
            src, dst, deep_send.at[phase, k], deep_recv.at[phase, k], device_id=partner, device_id_type=MESH
        )

    def deep_fine(phase, cur):
        copy = deep_copy(cur.at[pl.ds(0, 3), mine_f], cur.at[pl.ds(0, 3), theirs_f], phase, 0)
        copy.start()
        return copy

    def deep_coarse(phase, cur):
        copy = deep_copy(cur.at[pl.ds(0, 3), mine_c], cur.at[pl.ds(0, 3), theirs_c], phase, 1)
        copy.start()
        return copy

    def deep_interface(phase, cur_f, cur_c):
        copy = deep_copy(give.at[phase], got.at[phase], phase, 2)

        @pl.when(top)
        def _():
            for c in range(3):
                give[phase, c] = cur_c[c, 1]

        @pl.when(jnp.logical_not(top))
        def _():
            fine = jnp.concatenate([cur_f[c, FL] for c in range(3)], axis=0)
            small = times_left(rows_down[...], times_right(fine, lanes_down[...]))
            for c in range(3):
                give[phase, c] = small[c * CR : (c + 1) * CR]

        copy.start()
        return copy

    def deep_arrived(phase, copies, cur_f, cur_c):
        for copy in copies:
            copy.wait_recv()

        @pl.when(top)
        def _():
            for c in range(3):
                cur_c[c, 0] = got[phase, c]

        @pl.when(jnp.logical_not(top))
        def _():
            coarse = jnp.concatenate([got[phase, c] for c in range(3)], axis=0)
            large = times_left(rows_up[...], times_right(coarse, lanes_up[...]))
            for c in range(3):
                cur_f[c, FL + 1] = large[c * FR : (c + 1) * FR]

    def keep_f(c, slot, value):
        u1f[c, slot] = value

    def keep_c(c, slot, value):
        u1c[c, slot] = value

    def out_f(c, slot, value):
        fine_out[c, slot - 1] = value

    def out_c(c, slot, value):
        coarse_out[c, slot - 1] = value

    first_f = Step(FL, qf, qf, lambda c, s: qf[6 + c, s], 9, True, keep_f, (0, 0))
    first_c = Step(CL, qc, qc, lambda c, s: qc[5 + c, s], 8, False, keep_c, (0, 0))
    second_f = Step(FL, u1f, qf, lambda c, s: qf[c, s], 9, True, out_f, (8, 128))
    second_c = Step(CL, u1c, qc, lambda c, s: qc[c, s], 8, False, out_c, (8, 128))

    deep = [deep_fine(0, qf), deep_coarse(0, qc)]
    medium = [
        deep_copy(qf.at[pl.ds(3, 3), FL], qf.at[pl.ds(3, 3), 0], 0, 3),
        deep_copy(qc.at[pl.ds(3, 2), CL], qc.at[pl.ds(3, 2), 0], 0, 4),
    ]

    @pl.when(top)
    def _():
        for copy in medium:
            copy.start()
        for k in range(3, 5):
            qc[k, 0] = qc[k, 1]

    deep.append(deep_interface(0, qf, qc))
    first_f.inner()
    first_c.inner()
    deep_arrived(0, deep, qf, qc)

    @pl.when(jnp.logical_not(top))
    def _():
        for copy in medium:
            copy.wait_recv()

    first_f.outer()
    later = [deep_fine(1, u1f)]
    first_c.outer()
    later += [deep_coarse(1, u1c), deep_interface(1, u1f, u1c)]
    second_f.inner()
    second_c.inner()
    deep_arrived(1, later, u1f, u1c)
    second_f.outer()
    second_c.outer()

    for copy in deep + later:
        copy.wait_send()

    @pl.when(top)
    def _():
        for copy in medium:
            copy.wait_send()

    for k, copy in enumerate(sends):
        @pl.when(there[k][1])
        def _(copy=copy):
            copy.wait_send()


def per_device(*arrays):
    fine, coarse = arrays[0], arrays[3]
    return pl.pallas_call(
        kernel,
        out_shape=(pltpu.VMEM(fine.shape, F32), pltpu.VMEM(coarse.shape, F32)),
        in_specs=[pl.BlockSpec(memory_space=pltpu.HBM)] * 6,
        out_specs=(pl.BlockSpec(memory_space=pltpu.VMEM), pl.BlockSpec(memory_space=pltpu.VMEM)),
        scratch_shapes=[
            pltpu.VMEM((FQ, FL + 2, FR, FW), F32),
            pltpu.VMEM((CQ, CL + 2, CR, CW), F32),
            pltpu.VMEM((3, FL + 2, FR, FW), F32),
            pltpu.VMEM((3, CL + 2, CR, CW), F32),
            pltpu.VMEM((X_LOW_ROWS, 128), F32),
            pltpu.VMEM((X_ROWS, 128), F32),
            pltpu.VMEM((Y_ROWS + C_FINE, 128), F32),
            pltpu.VMEM((X_LOW_ROWS, 128), F32),
            pltpu.VMEM((X_ROWS, 128), F32),
            pltpu.VMEM((2, Y_ROWS, 128), F32),
            pltpu.VMEM((4, C_ROWS, 128), F32),
            pltpu.VMEM((STEPS, 3, CR, CW), F32),
            pltpu.VMEM((STEPS, 3, CR, CW), F32),
            pltpu.VMEM((FW, CW), BF16),
            pltpu.VMEM((CW, FW), BF16),
            pltpu.VMEM((3 * CR, 3 * FR), BF16),
            pltpu.VMEM((3 * FR, 3 * CR), BF16),
            pltpu.SemaphoreType.DMA((8,)),
            pltpu.SemaphoreType.DMA((8,)),
            pltpu.SemaphoreType.DMA((8,)),
            pltpu.SemaphoreType.DMA((STEPS, 5)),
            pltpu.SemaphoreType.DMA((STEPS, 5)),
        ],
        compiler_params=pltpu.CompilerParams(
            collective_id=0, has_side_effects=True, vmem_limit_bytes=40 * 2**20
        ),
    )(*[pltpu.with_memory_space_constraint(a, pltpu.HBM) for a in arrays])


def solution(mesh):
    spec = P(None, "dev", "gx", "gy")
    return jax.shard_map(
        per_device, mesh=mesh, in_specs=(spec,) * 6, out_specs=(spec, spec), check_vma=False
    )
```

```python
import jax
import jax.numpy as jnp
from jax import lax
from jax.experimental import pallas as pl
from jax.experimental.pallas import tpu as pltpu
from jax.sharding import PartitionSpec as P

STEPS = 2
STEP_SQUARED = 0.15 * 0.15
MESH = pl.DeviceIdType.MESH
F32 = jnp.float32

FR, FW = 24, 384
CR, CW = 16, 256
FL, CL = 4, 8
FQ = 10
CQ = 9

X_FINE = FQ * 16
X_COARSE = 14 * 8
X_EXTRA = 3 * 16
X_ROWS = X_FINE + X_COARSE + X_EXTRA
X_LOW_ROWS = X_FINE + X_COARSE
Y_FINE = 32
Y_COARSE = 24
C_FINE = 16
Y_ROWS = Y_FINE + Y_COARSE
C_ROWS = Y_COARSE + C_FINE
SIDES = ((-1, 0), (1, 0), (0, -1), (0, 1), (-1, -1), (-1, 1), (1, -1), (1, 1))


def iota(shape, dim):
    return lax.broadcasted_iota(jnp.int32, shape, dim)


def turned(value, shift, axis):
    shift = shift % value.shape[axis]
    return pltpu.roll(value, shift, axis) if shift else value


def picked(tile, index, axis):
    return jnp.take_along_axis(tile, index, axis=axis)


def restrict(tiles):
    row, lane = iota((8, 128), 0), iota((8, 128), 1)
    row_at, lane_at = (2 * row) & 7, (2 * lane) & 127

    def pairs(tile, axis, at):
        return picked(tile + turned(tile, -1, axis), at, axis)

    def joined(halo, first, second, half, at):
        return halo, jnp.where(at < half, first, second)

    columns = []
    for w in range(3):
        columns.append(joined(*[pairs(tiles(r, w), 0, row_at) for r in range(3)], 4, row))
    out = []
    for r in range(2):
        out.append(joined(*[0.25 * pairs(columns[w][r], 1, lane_at) for w in range(3)], 64, lane))
    return out


def prolong(tiles):
    row, lane = iota((8, 128), 0), iota((8, 128), 1)

    def spread(halo, own, half, at, axis):
        low = at // 2
        return (
            picked(halo, jnp.where(at < half, low, low + half), axis),
            picked(own, low, axis),
            picked(own, low + half, axis),
        )

    rows = [spread(tiles(r, 0), tiles(r, 1), 64, lane, 1) for r in range(2)]
    columns = [spread(rows[0][w], rows[1][w], 4, row, 0) for w in range(3)]
    return [[columns[w][r] for w in range(3)] for r in range(3)]


def gradients_to_stress(here, below, medium, stretch, which):
    def ahead(value, axis):
        return turned(value, -1, axis)

    mu, lam = medium
    dz = [b - h for b, h in zip(below, here)]
    if stretch is not None:
        dz = [d * stretch for d in dz]
    dx = [ahead(h, 0) - h for h in here]
    dy = [ahead(h, 1) - h for h in here]
    bulk = lam * (dx[0] + dy[1] + dz[2])
    twice = mu + mu
    out = {"zz": bulk + twice * dz[2], "xz": mu * (dz[0] + dx[2]), "yz": mu * (dz[1] + dy[2])}
    if which == "all":
        out["xx"] = bulk + twice * dx[0]
        out["yy"] = bulk + twice * dy[1]
        out["xy"] = mu * (dy[0] + dx[1])
    return out


class Step:
    def __init__(self, count, cur, qty, before_at, scale_at, stretched, write, crop):
        self.count, self.cur, self.qty, self.before_at = count, cur, qty, before_at
        self.scale_at, self.stretched, self.write, self.crop = scale_at, stretched, write, crop

    def cut(self, value):
        return value[self.crop[0] :, self.crop[1] :]

    def stress(self, slot, which="all"):
        cur, qty = self.cur, self.qty
        stretch = qty[5, slot] if self.stretched else None
        return gradients_to_stress(
            [cur[c, slot] for c in range(3)],
            [cur[c, slot + 1] for c in range(3)],
            (qty[3, slot], qty[4, slot]),
            stretch,
            which,
        )

    def move(self, slot, s, above):
        cut = self.cut

        def back_x(name):
            return cut(s[name]) - cut(turned(s[name], 1, 0))

        def back_y(name):
            return cut(s[name]) - cut(turned(s[name], 1, 1))

        def back_z(name):
            d = cut(s[name]) - cut(above[name])
            return d * cut(self.qty[5, slot]) if self.stretched else d

        force = (
            back_x("xx") + back_y("xy") + back_z("xz"),
            back_x("xy") + back_y("yy") + back_z("yz"),
            back_x("xz") + back_y("yz") + back_z("zz"),
        )
        scale = cut(self.qty[self.scale_at, slot])
        for c in range(3):
            now = cut(self.cur[c, slot])
            before = cut(self.before_at(c, slot))
            self.write(c, slot, now + now - before + scale * force[c])

    def inner(self):
        self.first = above = self.stress(1)
        for slot in range(2, self.count):
            s = self.stress(slot)
            self.move(slot, s, above)
            above = s
        self.above = above

    def outer(self):
        last = self.stress(self.count)
        self.move(self.count, last, self.above)
        self.move(1, self.first, self.stress(0, "vertical"))


def pack_x(qf, qc, low, high):
    row8 = iota((8, 256), 0)
    crow = iota((8, 128), 0)

    def store(ref, at, value):
        ref[pl.ds(at, 8), :] = value[:, :128]
        ref[pl.ds(at + 8, 8), :] = value[:, 128:]

    for g in range(FQ):
        up = jnp.zeros((8, 256), F32)
        down = up
        for l in range(FL):
            z = jnp.where(row8 < 4, qf[g, l + 1, 8:16, 128:], qf[g, l + 1, 16:24, 128:])
            t = turned(z, 2 * l, 0)
            up = t if l == 0 else jnp.where(row8 // 2 == l, t, up)
            down = t if l == 0 else jnp.where(row8 // 2 == l - 1, t, down)
        store(high, g * 16, up)
        store(low, g * 16, down)
    for q in range(5):
        for half in range(2):
            for l in range(4):
                t = turned(qc[q, half * 4 + l + 1, 8:16, 128:], 2 * l, 0)
                up = t if l == 0 else jnp.where(crow // 2 == l, t, up)
                down = t if l == 0 else jnp.where(crow // 2 == l - 1, t, down)
            at = X_FINE + (q * 2 + half) * 8
            high[pl.ds(at, 8), :] = up
            low[pl.ds(at, 8), :] = down
    for q in range(4):
        for l in range(8):
            t = turned(qc[5 + q, l + 1, 8:16, 128:], l, 0)
            up = t if l == 0 else jnp.where(crow == l, t, up)
            down = t if l == 0 else jnp.where(crow == l - 1, t, down)
        at = X_FINE + (10 + q) * 8
        high[pl.ds(at, 8), :] = up
        low[pl.ds(at, 8), :] = down
    for c in range(3):
        more = jnp.where(row8 < 2, turned(qf[c, 3, 8:16, 128:], -2, 0), qf[c, 4, 8:16, 128:])
        store(high, X_FINE + X_COARSE + c * 16, more)


def unpack_x(qf, qc, low, high):
    row8 = iota((8, 256), 0)
    crow = iota((8, 128), 0)

    def load(ref, at):
        return jnp.concatenate([ref[pl.ds(at, 8), :], ref[pl.ds(at + 8, 8), :]], axis=1)

    for g in range(FQ):
        up = load(high, g * 16)
        down = load(low, g * 16)
        more = load(high, X_FINE + X_COARSE + g * 16) if g < 3 else None
        for l in range(FL):
            t = jnp.where(row8 < 4, turned(up, -2 * l, 0), turned(down, -2 * l, 0))
            if g < 3 and l == 2:
                t = jnp.where(row8 // 2 == 1, turned(more, 2, 0), t)
            if g < 3 and l == 3:
                t = jnp.where(row8 // 2 == 1, more, t)
            qf[g, l + 1, 0:8, 128:] = t
    for q in range(5):
        for half in range(2):
            at = X_FINE + (q * 2 + half) * 8
            up = high[pl.ds(at, 8), :]
            down = low[pl.ds(at, 8), :]
            for l in range(4):
                t = jnp.where(crow < 4, turned(up, -2 * l, 0), turned(down, -2 * l, 0))
                qc[q, half * 4 + l + 1, 0:8, 128:] = t
    for q in range(4):
        at = X_FINE + (10 + q) * 8
        up = high[pl.ds(at, 8), :]
        down = low[pl.ds(at, 8), :]
        for l in range(8):
            qc[5 + q, l + 1, 0:8, 128:] = jnp.where(crow < 4, turned(up, -l, 0), turned(down, -l, 0))


def pack_y(qf, qc, out):
    lane = iota((16, 128), 1)
    lane8 = iota((8, 128), 1)
    row8 = iota((8, 128), 0)
    for t in range(2):
        packed = jnp.zeros((16, 128), F32)
        for k in range(20):
            g, l = t * 5 + k // 4, k % 4
            z = jnp.where(lane < 64, qf[g, l + 1, 8:24, 128:256], qf[g, l + 1, 8:24, 256:384])
            mine = ((lane + (2 - 6 * k + 128)) & 127) < 6
            packed = jnp.where(mine, turned(z, 6 * k, 1), packed)
        out[pl.ds(t * 16, 16), :] = packed
        out[pl.ds(Y_ROWS + t * 8, 8), :] = jnp.where(row8 < 4, packed[:8], packed[8:])
    for t in range(3):
        packed = jnp.zeros((8, 128), F32)
        for k in range(32 if t < 2 else 8):
            q, l = t * 4 + k // 8, k % 8
            mine = ((lane8 + (2 - 4 * k + 128)) & 127) < 4
            packed = jnp.where(mine, turned(qc[q, l + 1, 8:16, 128:256], 4 * k, 1), packed)
        out[pl.ds(Y_FINE + t * 8, 8), :] = packed


def unpack_y(qf, qc, side, corner):
    lane = iota((16, 128), 1)
    lane8 = iota((8, 128), 1)
    row8 = iota((8, 128), 0)
    fine_low = ((lane + 2) & 127) % 6 < 2
    fine_low8 = ((lane8 + 2) & 127) % 6 < 2
    coarse_low8 = ((lane8 + 2) & 127) % 4 < 2

    def corners(at, low):
        before = jnp.where(low, corner[0, pl.ds(at, 8), :], corner[1, pl.ds(at, 8), :])
        after = jnp.where(low, corner[2, pl.ds(at, 8), :], corner[3, pl.ds(at, 8), :])
        return jnp.where(row8 < 4, after, before)

    for t in range(2):
        own = jnp.where(fine_low, side[0, pl.ds(t * 16, 16), :], side[1, pl.ds(t * 16, 16), :])
        both = jnp.concatenate([corners(Y_COARSE + t * 8, fine_low8), own], axis=0)
        for k in range(20):
            g, l = t * 5 + k // 4, k % 4
            qf[g, l + 1, :, 0:128] = turned(both, -6 * k, 1)
    for t in range(3):
        at = Y_FINE + t * 8
        own = jnp.where(coarse_low8, side[0, pl.ds(at, 8), :], side[1, pl.ds(at, 8), :])
        both = jnp.concatenate([corners(t * 8, coarse_low8), own], axis=0)
        for k in range(32 if t < 2 else 8):
            q, l = t * 4 + k // 8, k % 8
            qc[q, l + 1, :, 0:128] = turned(both, -4 * k, 1)


def kernel(
    fine_now, fine_before, fine_material, coarse_now, coarse_before, coarse_material,
    fine_out, coarse_out,
    qf, qc, u1f, u1c,
    sx_low, sx_high, sy, rx_low, rx_high, ry, rc,
    give, got,
    load_sem, send_sem, recv_sem, deep_send, deep_recv,
):
    gx, gy, dev = lax.axis_index("gx"), lax.axis_index("gy"), lax.axis_index("dev")
    nx, ny = lax.axis_size("gx"), lax.axis_size("gy")
    top = dev == 0
    partner = {"gx": gx, "gy": gy, "dev": 1 - dev}
    there = []
    for dx, dy in SIDES:
        x, y = gx + dx, gy + dy
        there.append(({"gx": x, "gy": y, "dev": dev}, (x >= 0) & (x < nx) & (y >= 0) & (y < ny)))

    barrier = pltpu.get_barrier_semaphore()
    expected = 1
    pl.semaphore_signal(barrier, inc=1, device_id=partner, device_id_type=MESH)
    for where, present in there:
        @pl.when(present)
        def _(where=where):
            pl.semaphore_signal(barrier, inc=1, device_id=where, device_id_type=MESH)
        expected = expected + jnp.where(present, 1, 0)

    fine_own = (pl.ds(1, FL), pl.ds(8, 16), pl.ds(128, 256))
    coarse_own = (pl.ds(1, CL), pl.ds(8, 8), pl.ds(128, 128))
    loads = [
        (fine_now, qf.at[(pl.ds(0, 3), *fine_own)]),
        (fine_material.at[pl.ds(1, 3)], qf.at[(pl.ds(3, 3), *fine_own)]),
        (fine_before, qf.at[(pl.ds(6, 3), *fine_own)]),
        (fine_material.at[pl.ds(0, 1)], qf.at[(pl.ds(9, 1), *fine_own)]),
        (coarse_now, qc.at[(pl.ds(0, 3), *coarse_own)]),
        (coarse_material.at[pl.ds(1, 2)], qc.at[(pl.ds(3, 2), *coarse_own)]),
        (coarse_before, qc.at[(pl.ds(5, 3), *coarse_own)]),
        (coarse_material.at[pl.ds(0, 1)], qc.at[(pl.ds(8, 1), *coarse_own)]),
    ]
    copies = [pltpu.make_async_copy(src, dst, load_sem.at[k]) for k, (src, dst) in enumerate(loads)]
    for copy in copies:
        copy.start()

    def zero_unless(present, ref, at=None):
        @pl.when(jnp.logical_not(present))
        def _():
            if at is None:
                ref[...] = jnp.zeros(ref.shape, F32)
            else:
                ref[at] = jnp.zeros(ref.shape[1:], F32)

    zero_unless(there[0][1], rx_low)
    zero_unless(there[1][1], rx_high)
    for k in range(2):
        zero_unless(there[2 + k][1], ry, k)
    for k in range(4):
        zero_unless(there[4 + k][1], rc, k)

    @pl.when(top)
    def _():
        for c in range(3):
            qf[c, 0] = jnp.zeros((FR, FW), F32)
            u1f[c, 0] = jnp.zeros((FR, FW), F32)
        for k in range(3, 6):
            qf[k, 0] = jnp.zeros((FR, FW), F32)

    @pl.when(jnp.logical_not(top))
    def _():
        for c in range(3):
            qc[c, CL + 1] = jnp.zeros((CR, CW), F32)
            u1c[c, CL + 1] = jnp.zeros((CR, CW), F32)

    for copy in copies:
        copy.wait()
    for l in range(FL):
        own = (9, l + 1, pl.ds(8, 16), pl.ds(128, 256))
        qf[own] = STEP_SQUARED / qf[own]
    for l in range(CL):
        own = (8, l + 1, pl.ds(8, 8), pl.ds(128, 128))
        qc[own] = (0.25 * STEP_SQUARED) / qc[own]
    pack_x(qf, qc, sx_low, sx_high)
    pack_y(qf, qc, sy)
    pl.semaphore_wait(barrier, expected)

    side_msg, corner_msg = sy.at[pl.ds(0, Y_ROWS)], sy.at[pl.ds(Y_FINE, C_ROWS)]
    messages = [
        (sx_high, rx_high), (sx_low, rx_low), (side_msg, ry.at[1]), (side_msg, ry.at[0]),
        (corner_msg, rc.at[3]), (corner_msg, rc.at[2]), (corner_msg, rc.at[1]), (corner_msg, rc.at[0]),
    ]
    sends = []
    for k, (src, dst) in enumerate(messages):
        copy = pltpu.make_async_remote_copy(
            src, dst, send_sem.at[k], recv_sem.at[k], device_id=there[k][0], device_id_type=MESH
        )

        @pl.when(there[k][1])
        def _(copy=copy):
            copy.start()

        sends.append(copy)

    def arrived(k):
        opposite = SIDES.index((-SIDES[k][0], -SIDES[k][1]))

        @pl.when(there[opposite][1])
        def _():
            sends[k].wait_recv()

    for k in range(8):
        arrived(k)
    unpack_x(qf, qc, rx_low, rx_high)
    unpack_y(qf, qc, ry, rc)

    mine_f, theirs_f = jnp.where(top, FL, 1), jnp.where(top, 0, FL + 1)
    mine_c, theirs_c = jnp.where(top, CL, 1), jnp.where(top, 0, CL + 1)

    def deep_copy(src, dst, phase, k):
        return pltpu.make_async_remote_copy(
            src, dst, deep_send.at[phase, k], deep_recv.at[phase, k], device_id=partner, device_id_type=MESH
        )

    def deep_fine(phase, cur):
        copy = deep_copy(cur.at[pl.ds(0, 3), mine_f], cur.at[pl.ds(0, 3), theirs_f], phase, 0)
        copy.start()
        return copy

    def deep_coarse(phase, cur):
        copy = deep_copy(cur.at[pl.ds(0, 3), mine_c], cur.at[pl.ds(0, 3), theirs_c], phase, 1)
        copy.start()
        return copy

    def deep_interface(phase, cur_f, cur_c):
        copy = deep_copy(give.at[phase], got.at[phase], phase, 2)

        @pl.when(top)
        def _():
            for c in range(3):
                give[phase, c] = cur_c[c, 1]

        @pl.when(jnp.logical_not(top))
        def _():
            for c in range(3):
                small = restrict(lambda r, w: cur_f[c, FL, 8 * r : 8 * r + 8, 128 * w : 128 * w + 128])
                for r in range(2):
                    for w in range(2):
                        give[phase, c, 8 * r : 8 * r + 8, 128 * w : 128 * w + 128] = small[r][w]

        copy.start()
        return copy

    def deep_arrived(phase, copies, cur_f, cur_c):
        for copy in copies:
            copy.wait_recv()

        @pl.when(top)
        def _():
            for c in range(3):
                cur_c[c, 0] = got[phase, c]

        @pl.when(jnp.logical_not(top))
        def _():
            for c in range(3):
                large = prolong(lambda r, w: got[phase, c, 8 * r : 8 * r + 8, 128 * w : 128 * w + 128])
                for r in range(3):
                    for w in range(3):
                        cur_f[c, FL + 1, 8 * r : 8 * r + 8, 128 * w : 128 * w + 128] = large[r][w]

    def keep_f(c, slot, value):
        u1f[c, slot] = value

    def keep_c(c, slot, value):
        u1c[c, slot] = value

    def out_f(c, slot, value):
        fine_out[c, slot - 1] = value

    def out_c(c, slot, value):
        coarse_out[c, slot - 1] = value

    first_f = Step(FL, qf, qf, lambda c, s: qf[6 + c, s], 9, True, keep_f, (0, 0))
    first_c = Step(CL, qc, qc, lambda c, s: qc[5 + c, s], 8, False, keep_c, (0, 0))
    second_f = Step(FL, u1f, qf, lambda c, s: qf[c, s], 9, True, out_f, (8, 128))
    second_c = Step(CL, u1c, qc, lambda c, s: qc[c, s], 8, False, out_c, (8, 128))

    deep = [deep_fine(0, qf), deep_coarse(0, qc)]
    medium = [
        deep_copy(qf.at[pl.ds(3, 3), FL], qf.at[pl.ds(3, 3), 0], 0, 3),
        deep_copy(qc.at[pl.ds(3, 2), CL], qc.at[pl.ds(3, 2), 0], 0, 4),
    ]

    @pl.when(top)
    def _():
        for copy in medium:
            copy.start()
        for k in range(3, 5):
            qc[k, 0] = qc[k, 1]

    deep.append(deep_interface(0, qf, qc))
    first_f.inner()
    first_c.inner()
    deep_arrived(0, deep, qf, qc)

    @pl.when(jnp.logical_not(top))
    def _():
        for copy in medium:
            copy.wait_recv()

    first_f.outer()
    later = [deep_fine(1, u1f)]
    first_c.outer()
    later += [deep_coarse(1, u1c), deep_interface(1, u1f, u1c)]
    second_f.inner()
    second_c.inner()
    deep_arrived(1, later, u1f, u1c)
    second_f.outer()
    second_c.outer()

    for copy in deep + later:
        copy.wait_send()

    @pl.when(top)
    def _():
        for copy in medium:
            copy.wait_send()

    for k, copy in enumerate(sends):
        @pl.when(there[k][1])
        def _(copy=copy):
            copy.wait_send()


def store(fine, coarse, fine_out, coarse_out, sems):
    copies = [pltpu.make_async_copy(fine, fine_out, sems.at[0]), pltpu.make_async_copy(coarse, coarse_out, sems.at[1])]
    for copy in copies:
        copy.start()
    for copy in copies:
        copy.wait()


def per_device(*arrays):
    fine, coarse = arrays[0], arrays[3]
    after = stepped(arrays, fine, coarse)
    return pl.pallas_call(
        store,
        out_shape=(jax.ShapeDtypeStruct(fine.shape, F32), jax.ShapeDtypeStruct(coarse.shape, F32)),
        in_specs=[pl.BlockSpec(memory_space=pltpu.VMEM)] * 2,
        out_specs=(pl.BlockSpec(memory_space=pltpu.HBM), pl.BlockSpec(memory_space=pltpu.HBM)),
        scratch_shapes=[pltpu.SemaphoreType.DMA((2,))],
    )(*[pltpu.with_memory_space_constraint(a, pltpu.VMEM) for a in after])


def stepped(arrays, fine, coarse):
    return pl.pallas_call(
        kernel,
        out_shape=(pltpu.VMEM(fine.shape, F32), pltpu.VMEM(coarse.shape, F32)),
        in_specs=[pl.BlockSpec(memory_space=pltpu.HBM)] * 6,
        out_specs=(pl.BlockSpec(memory_space=pltpu.VMEM), pl.BlockSpec(memory_space=pltpu.VMEM)),
        scratch_shapes=[
            pltpu.VMEM((FQ, FL + 2, FR, FW), F32),
            pltpu.VMEM((CQ, CL + 2, CR, CW), F32),
            pltpu.VMEM((3, FL + 2, FR, FW), F32),
            pltpu.VMEM((3, CL + 2, CR, CW), F32),
            pltpu.VMEM((X_LOW_ROWS, 128), F32),
            pltpu.VMEM((X_ROWS, 128), F32),
            pltpu.VMEM((Y_ROWS + C_FINE, 128), F32),
            pltpu.VMEM((X_LOW_ROWS, 128), F32),
            pltpu.VMEM((X_ROWS, 128), F32),
            pltpu.VMEM((2, Y_ROWS, 128), F32),
            pltpu.VMEM((4, C_ROWS, 128), F32),
            pltpu.VMEM((STEPS, 3, CR, CW), F32),
            pltpu.VMEM((STEPS, 3, CR, CW), F32),
            pltpu.SemaphoreType.DMA((8,)),
            pltpu.SemaphoreType.DMA((8,)),
            pltpu.SemaphoreType.DMA((8,)),
            pltpu.SemaphoreType.DMA((STEPS, 5)),
            pltpu.SemaphoreType.DMA((STEPS, 5)),
        ],
        compiler_params=pltpu.CompilerParams(
            collective_id=0, has_side_effects=True, vmem_limit_bytes=40 * 2**20
        ),
    )(*[pltpu.with_memory_space_constraint(a, pltpu.HBM) for a in arrays])


def solution(mesh):
    spec = P(None, "dev", "gx", "gy")
    return jax.shard_map(
        per_device, mesh=mesh, in_specs=(spec,) * 6, out_specs=(spec, spec), check_vma=False
    )
```

```python
import jax
import jax.numpy as jnp
from jax import lax
from jax.experimental import pallas as pl
from jax.experimental.pallas import tpu as pltpu
from jax.sharding import PartitionSpec as P

STEPS = 2
STEP_SQUARED = 0.15 * 0.15
MESH = pl.DeviceIdType.MESH
F32 = jnp.float32

FR, FW = 24, 384
CR, CW = 16, 256
FL, CL = 4, 8
FQ = 10
CQ = 9

X_COARSE = 6 * 16
X_EXTRA = X_COARSE + 10 * 8
X_LOW_FIRST = X_EXTRA
X_HIGH_FIRST = X_EXTRA + 3 * 16
X_REST = 4 * 16 + 4 * 8
X_LOW_ROWS = X_LOW_FIRST + X_REST
X_ROWS = X_HIGH_FIRST + X_REST
Y_FINE = 32
Y_COARSE = 24
C_FINE = 16
Y_ROWS = Y_FINE + Y_COARSE
C_ROWS = Y_COARSE + C_FINE
SIDES = ((-1, 0), (1, 0), (0, -1), (0, 1), (-1, -1), (-1, 1), (1, -1), (1, 1))


def iota(shape, dim):
    return lax.broadcasted_iota(jnp.int32, shape, dim)


def turned(value, shift, axis):
    shift = shift % value.shape[axis]
    return pltpu.roll(value, shift, axis) if shift else value


def picked(tile, index, axis):
    return jnp.take_along_axis(tile, index, axis=axis)


def restrict(tiles, r, w):
    row, lane = iota((8, 128), 0), iota((8, 128), 1)
    row_at, lane_at = (2 * row) & 7, (2 * lane) & 127

    def pairs(tile, axis, at):
        return picked(tile + turned(tile, -1, axis), at, axis)

    def joined(values, half, at):
        return values[0] if len(values) == 1 else jnp.where(at < half, values[0], values[1])

    sources = ((0,), (1, 2))
    columns = [joined([pairs(tiles(a, b), 0, row_at) for a in sources[r]], 4, row) for b in sources[w]]
    return joined([0.25 * pairs(v, 1, lane_at) for v in columns], 64, lane)


def prolong(tiles):
    row, lane = iota((8, 128), 0), iota((8, 128), 1)

    def spread(halo, own, half, at, axis):
        low = at // 2
        return (
            picked(halo, jnp.where(at < half, low, low + half), axis),
            picked(own, low, axis),
            picked(own, low + half, axis),
        )

    rows = [spread(tiles(r, 0), tiles(r, 1), 64, lane, 1) for r in range(2)]
    columns = [spread(rows[0][w], rows[1][w], 4, row, 0) for w in range(3)]
    return [[columns[w][r] for w in range(3)] for r in range(3)]


def gradients_to_stress(here, below, medium, stretch, which):
    def ahead(value, axis):
        return turned(value, -1, axis)

    mu, lam = medium
    dz = [b - h for b, h in zip(below, here)]
    if stretch is not None:
        dz = [d * stretch for d in dz]
    dx = [ahead(h, 0) - h for h in here]
    dy = [ahead(h, 1) - h for h in here]
    bulk = lam * (dx[0] + dy[1] + dz[2])
    twice = mu + mu
    out = {"zz": bulk + twice * dz[2], "xz": mu * (dz[0] + dx[2]), "yz": mu * (dz[1] + dy[2])}
    if which == "all":
        out["xx"] = bulk + twice * dx[0]
        out["yy"] = bulk + twice * dy[1]
        out["xy"] = mu * (dy[0] + dx[1])
    return out


class Step:
    def __init__(self, count, cur, qty, before_at, scale_at, stretched, write, crop):
        self.count, self.cur, self.qty, self.before_at = count, cur, qty, before_at
        self.scale_at, self.stretched, self.write, self.crop = scale_at, stretched, write, crop

    def cut(self, value):
        return value[self.crop[0] :, self.crop[1] :]

    def stress(self, slot, which="all"):
        cur, qty = self.cur, self.qty
        stretch = qty[5, slot] if self.stretched else None
        return gradients_to_stress(
            [cur[c, slot] for c in range(3)],
            [cur[c, slot + 1] for c in range(3)],
            (qty[3, slot], qty[4, slot]),
            stretch,
            which,
        )

    def move(self, slot, s, above):
        cut = self.cut

        def back_x(name):
            return cut(s[name]) - cut(turned(s[name], 1, 0))

        def back_y(name):
            return cut(s[name]) - cut(turned(s[name], 1, 1))

        def back_z(name):
            d = cut(s[name]) - cut(above[name])
            return d * cut(self.qty[5, slot]) if self.stretched else d

        force = (
            back_x("xx") + back_y("xy") + back_z("xz"),
            back_x("xy") + back_y("yy") + back_z("yz"),
            back_x("xz") + back_y("yz") + back_z("zz"),
        )
        scale = cut(self.qty[self.scale_at, slot])
        for c in range(3):
            now = cut(self.cur[c, slot])
            before = cut(self.before_at(c, slot))
            self.write(c, slot, now + now - before + scale * force[c])

    def inner(self):
        self.first = above = self.stress(1)
        for slot in range(2, self.count):
            s = self.stress(slot)
            self.move(slot, s, above)
            above = s
        self.above = above

    def outer(self):
        last = self.stress(self.count)
        self.move(self.count, last, self.above)
        self.move(1, self.first, self.stress(0, "vertical"))


def fine_at(g, first):
    return g * 16 if g < 6 else first + (g - 6) * 16


def pack_x(qf, qc, low, high):
    row8 = iota((8, 256), 0)
    crow = iota((8, 128), 0)

    def store(ref, at, value):
        ref[pl.ds(at, 8), :] = value[:, :128]
        ref[pl.ds(at + 8, 8), :] = value[:, 128:]

    for g in range(FQ):
        up = jnp.zeros((8, 256), F32)
        down = up
        for l in range(FL):
            z = jnp.where(row8 < 4, qf[g, l + 1, 8:16, 128:], qf[g, l + 1, 16:24, 128:])
            t = turned(z, 2 * l, 0)
            up = t if l == 0 else jnp.where(row8 // 2 == l, t, up)
            down = t if l == 0 else jnp.where(row8 // 2 == l - 1, t, down)
        store(high, fine_at(g, X_HIGH_FIRST), up)
        store(low, fine_at(g, X_LOW_FIRST), down)
    for q in range(5):
        for half in range(2):
            for l in range(4):
                t = turned(qc[q, half * 4 + l + 1, 8:16, 128:], 2 * l, 0)
                up = t if l == 0 else jnp.where(crow // 2 == l, t, up)
                down = t if l == 0 else jnp.where(crow // 2 == l - 1, t, down)
            at = X_COARSE + (q * 2 + half) * 8
            high[pl.ds(at, 8), :] = up
            low[pl.ds(at, 8), :] = down
    for q in range(4):
        for l in range(8):
            t = turned(qc[5 + q, l + 1, 8:16, 128:], l, 0)
            up = t if l == 0 else jnp.where(crow == l, t, up)
            down = t if l == 0 else jnp.where(crow == l - 1, t, down)
        high[pl.ds(X_HIGH_FIRST + 64 + q * 8, 8), :] = up
        low[pl.ds(X_LOW_FIRST + 64 + q * 8, 8), :] = down
    for c in range(3):
        more = jnp.where(row8 < 2, turned(qf[c, 3, 8:16, 128:], -2, 0), qf[c, 4, 8:16, 128:])
        store(high, X_EXTRA + c * 16, more)


def unpack_x(qf, qc, low, high, first):
    row8 = iota((8, 256), 0)
    crow = iota((8, 128), 0)

    def load(ref, at):
        return jnp.concatenate([ref[pl.ds(at, 8), :], ref[pl.ds(at + 8, 8), :]], axis=1)

    for g in range(6) if first else range(6, FQ):
        up = load(high, fine_at(g, X_HIGH_FIRST))
        down = load(low, fine_at(g, X_LOW_FIRST))
        more = load(high, X_EXTRA + g * 16) if g < 3 else None
        for l in range(FL):
            t = jnp.where(row8 < 4, turned(up, -2 * l, 0), turned(down, -2 * l, 0))
            if g < 3 and l == 2:
                t = jnp.where(row8 // 2 == 1, turned(more, 2, 0), t)
            if g < 3 and l == 3:
                t = jnp.where(row8 // 2 == 1, more, t)
            qf[g, l + 1, 0:8, 128:] = t
    for q in range(5) if first else ():
        for half in range(2):
            at = X_COARSE + (q * 2 + half) * 8
            up = high[pl.ds(at, 8), :]
            down = low[pl.ds(at, 8), :]
            for l in range(4):
                t = jnp.where(crow < 4, turned(up, -2 * l, 0), turned(down, -2 * l, 0))
                qc[q, half * 4 + l + 1, 0:8, 128:] = t
    for q in () if first else range(4):
        up = high[pl.ds(X_HIGH_FIRST + 64 + q * 8, 8), :]
        down = low[pl.ds(X_LOW_FIRST + 64 + q * 8, 8), :]
        for l in range(8):
            qc[5 + q, l + 1, 0:8, 128:] = jnp.where(crow < 4, turned(up, -l, 0), turned(down, -l, 0))


def pack_y(qf, qc, out):
    lane = iota((16, 128), 1)
    lane8 = iota((8, 128), 1)
    row8 = iota((8, 128), 0)
    for t in range(2):
        packed = jnp.zeros((16, 128), F32)
        for k in range(20):
            g, l = t * 5 + k // 4, k % 4
            z = jnp.where(lane < 64, qf[g, l + 1, 8:24, 128:256], qf[g, l + 1, 8:24, 256:384])
            mine = ((lane + (2 - 6 * k + 128)) & 127) < 6
            packed = jnp.where(mine, turned(z, 6 * k, 1), packed)
        out[pl.ds(t * 16, 16), :] = packed
        out[pl.ds(Y_ROWS + t * 8, 8), :] = jnp.where(row8 < 4, packed[:8], packed[8:])
    for t in range(3):
        packed = jnp.zeros((8, 128), F32)
        for k in range(32 if t < 2 else 8):
            q, l = t * 4 + k // 8, k % 8
            mine = ((lane8 + (2 - 4 * k + 128)) & 127) < 4
            packed = jnp.where(mine, turned(qc[q, l + 1, 8:16, 128:256], 4 * k, 1), packed)
        out[pl.ds(Y_FINE + t * 8, 8), :] = packed


def unpack_y(qf, qc, side, corner):
    lane = iota((16, 128), 1)
    lane8 = iota((8, 128), 1)
    row8 = iota((8, 128), 0)
    fine_low = ((lane + 2) & 127) % 6 < 2
    fine_low8 = ((lane8 + 2) & 127) % 6 < 2
    coarse_low8 = ((lane8 + 2) & 127) % 4 < 2

    def corners(at, low):
        before = jnp.where(low, corner[0, pl.ds(at, 8), :], corner[1, pl.ds(at, 8), :])
        after = jnp.where(low, corner[2, pl.ds(at, 8), :], corner[3, pl.ds(at, 8), :])
        return jnp.where(row8 < 4, after, before)

    for t in range(2):
        own = jnp.where(fine_low, side[0, pl.ds(t * 16, 16), :], side[1, pl.ds(t * 16, 16), :])
        both = jnp.concatenate([corners(Y_COARSE + t * 8, fine_low8), own], axis=0)
        for k in range(20):
            g, l = t * 5 + k // 4, k % 4
            qf[g, l + 1, :, 0:128] = turned(both, -6 * k, 1)
    for t in range(3):
        at = Y_FINE + t * 8
        own = jnp.where(coarse_low8, side[0, pl.ds(at, 8), :], side[1, pl.ds(at, 8), :])
        both = jnp.concatenate([corners(t * 8, coarse_low8), own], axis=0)
        for k in range(32 if t < 2 else 8):
            q, l = t * 4 + k // 8, k % 8
            qc[q, l + 1, :, 0:128] = turned(both, -4 * k, 1)


def kernel(
    fine_now, fine_before, fine_material, coarse_now, coarse_before, coarse_material,
    fine_out, coarse_out,
    qf, qc, u1f, u1c,
    sx_low, sx_high, sy, rx_low, rx_high, ry, rc,
    give, got,
    load_sem, send_sem, recv_sem, deep_send, deep_recv,
):
    gx, gy, dev = lax.axis_index("gx"), lax.axis_index("gy"), lax.axis_index("dev")
    nx, ny = lax.axis_size("gx"), lax.axis_size("gy")
    top = dev == 0
    partner = {"gx": gx, "gy": gy, "dev": 1 - dev}
    there = []
    for dx, dy in SIDES:
        x, y = gx + dx, gy + dy
        there.append(({"gx": x, "gy": y, "dev": dev}, (x >= 0) & (x < nx) & (y >= 0) & (y < ny)))

    barrier = pltpu.get_barrier_semaphore()
    expected = 1
    pl.semaphore_signal(barrier, inc=1, device_id=partner, device_id_type=MESH)
    for where, present in there:
        @pl.when(present)
        def _(where=where):
            pl.semaphore_signal(barrier, inc=1, device_id=where, device_id_type=MESH)
        expected = expected + jnp.where(present, 1, 0)

    fine_own = (pl.ds(1, FL), pl.ds(8, 16), pl.ds(128, 256))
    coarse_own = (pl.ds(1, CL), pl.ds(8, 8), pl.ds(128, 128))
    loads = [
        (fine_now, qf.at[(pl.ds(0, 3), *fine_own)]),
        (fine_material.at[pl.ds(1, 3)], qf.at[(pl.ds(3, 3), *fine_own)]),
        (fine_before, qf.at[(pl.ds(6, 3), *fine_own)]),
        (fine_material.at[pl.ds(0, 1)], qf.at[(pl.ds(9, 1), *fine_own)]),
        (coarse_now, qc.at[(pl.ds(0, 3), *coarse_own)]),
        (coarse_material.at[pl.ds(1, 2)], qc.at[(pl.ds(3, 2), *coarse_own)]),
        (coarse_before, qc.at[(pl.ds(5, 3), *coarse_own)]),
        (coarse_material.at[pl.ds(0, 1)], qc.at[(pl.ds(8, 1), *coarse_own)]),
    ]
    copies = [pltpu.make_async_copy(src, dst, load_sem.at[k]) for k, (src, dst) in enumerate(loads)]
    for copy in copies:
        copy.start()

    def zero_unless(present, ref, at=None):
        @pl.when(jnp.logical_not(present))
        def _():
            if at is None:
                ref[...] = jnp.zeros(ref.shape, F32)
            else:
                ref[at] = jnp.zeros(ref.shape[1:], F32)

    zero_unless(there[0][1], rx_low)
    zero_unless(there[1][1], rx_high)
    for k in range(2):
        zero_unless(there[2 + k][1], ry, k)
    for k in range(4):
        zero_unless(there[4 + k][1], rc, k)

    @pl.when(top)
    def _():
        for c in range(3):
            qf[c, 0] = jnp.zeros((FR, FW), F32)
            u1f[c, 0] = jnp.zeros((FR, FW), F32)
        for k in range(3, 6):
            qf[k, 0] = jnp.zeros((FR, FW), F32)

    @pl.when(jnp.logical_not(top))
    def _():
        for c in range(3):
            qc[c, CL + 1] = jnp.zeros((CR, CW), F32)
            u1c[c, CL + 1] = jnp.zeros((CR, CW), F32)

    for copy in copies:
        copy.wait()
    for l in range(FL):
        own = (9, l + 1, pl.ds(8, 16), pl.ds(128, 256))
        qf[own] = STEP_SQUARED / qf[own]
    for l in range(CL):
        own = (8, l + 1, pl.ds(8, 8), pl.ds(128, 128))
        qc[own] = (0.25 * STEP_SQUARED) / qc[own]
    pack_x(qf, qc, sx_low, sx_high)
    pack_y(qf, qc, sy)

    areas = (
        ((pl.ds(8, 16), pl.ds(128, 256)), (pl.ds(8, 8), pl.ds(128, 128)), ((1, 1),)),
        ((pl.ds(0, FR), pl.ds(0, 128)), (pl.ds(0, CR), pl.ds(0, 128)), ((0, 0), (1, 0))),
        ((pl.ds(0, 8), pl.ds(128, 256)), (pl.ds(0, 8), pl.ds(128, 128)), ((0, 1),)),
    )

    def deep_copy(src, dst, phase, k):
        return pltpu.make_async_remote_copy(
            src, dst, deep_send.at[phase, k], deep_recv.at[phase, k], device_id=partner, device_id_type=MESH
        )

    def restricted(phase, cur_f, places):
        @pl.when(jnp.logical_not(top))
        def _():
            for c in range(3):
                for r, w in places:
                    give[phase, c, 8 * r : 8 * r + 8, 128 * w : 128 * w + 128] = restrict(
                        lambda a, b: cur_f[c, FL, 8 * a : 8 * a + 8, 128 * b : 128 * b + 128], r, w
                    )

    from_top, from_bottom = [], []
    for part, (fine, coarse, _) in enumerate(areas):
        from_top.append(
            [
                deep_copy(qf.at[(pl.ds(0, 6), FL, *fine)], qf.at[(pl.ds(0, 6), 0, *fine)], 0, part * 3),
                deep_copy(qc.at[(pl.ds(0, 5), CL, *coarse)], qc.at[(pl.ds(0, 5), 0, *coarse)], 0, part * 3 + 1),
                deep_copy(qc.at[(pl.ds(0, 3), 1, *coarse)], got.at[(0, pl.ds(0, 3), *coarse)], 0, part * 3 + 2),
            ]
        )
        from_bottom.append(
            [
                deep_copy(qf.at[(pl.ds(0, 3), 1, *fine)], qf.at[(pl.ds(0, 3), FL + 1, *fine)], 0, part * 3),
                deep_copy(qc.at[(pl.ds(0, 3), 1, *coarse)], qc.at[(pl.ds(0, 3), CL + 1, *coarse)], 0, part * 3 + 1),
                deep_copy(give.at[(0, pl.ds(0, 3), *coarse)], qc.at[(pl.ds(0, 3), 0, *coarse)], 0, part * 3 + 2),
            ]
        )

    def start_part(part):
        @pl.when(top)
        def _():
            for copy in from_top[part]:
                copy.start()

        @pl.when(jnp.logical_not(top))
        def _():
            for copy in from_bottom[part]:
                copy.start()

    restricted(0, qf, areas[0][2])
    pl.semaphore_wait(barrier, expected)

    side_msg, corner_msg = sy.at[pl.ds(0, Y_ROWS)], sy.at[pl.ds(Y_FINE, C_ROWS)]
    high_first, high_rest = pl.ds(0, X_HIGH_FIRST), pl.ds(X_HIGH_FIRST, X_REST)
    low_first, low_rest = pl.ds(0, X_LOW_FIRST), pl.ds(X_LOW_FIRST, X_REST)
    messages = [
        (4, corner_msg, rc.at[3]), (5, corner_msg, rc.at[2]), (6, corner_msg, rc.at[1]), (7, corner_msg, rc.at[0]),
        (2, side_msg, ry.at[1]), (3, side_msg, ry.at[0]),
        (0, sx_high.at[high_first], rx_high.at[high_first]), (1, sx_low.at[low_first], rx_low.at[low_first]),
        (0, sx_high.at[high_rest], rx_high.at[high_rest]), (1, sx_low.at[low_rest], rx_low.at[low_rest]),
    ]
    sends = []
    for n, (k, src, dst) in enumerate(messages):
        copy = pltpu.make_async_remote_copy(
            src, dst, send_sem.at[n], recv_sem.at[n], device_id=there[k][0], device_id_type=MESH
        )

        @pl.when(there[k][1])
        def _(copy=copy):
            copy.start()

        sends.append((k, copy))

    def arrived(*numbers):
        for n in numbers:
            k, copy = sends[n]
            opposite = SIDES.index((-SIDES[k][0], -SIDES[k][1]))

            @pl.when(there[opposite][1])
            def _(copy=copy):
                copy.wait_recv()

    start_part(0)
    arrived(0, 1, 2, 3, 4, 5)
    unpack_y(qf, qc, ry, rc)
    restricted(0, qf, areas[1][2])
    start_part(1)
    arrived(6, 7)
    unpack_x(qf, qc, rx_low, rx_high, True)
    restricted(0, qf, areas[2][2])
    start_part(2)

    @pl.when(top)
    def _():
        for k in range(3, 5):
            qc[k, 0] = qc[k, 1]

    arrived(8, 9)
    unpack_x(qf, qc, rx_low, rx_high, False)

    def prolonged(phase, cur_f):
        for c in range(3):
            large = prolong(lambda r, w: got[phase, c, 8 * r : 8 * r + 8, 128 * w : 128 * w + 128])
            for r in range(3):
                for w in range(3):
                    cur_f[c, FL + 1, 8 * r : 8 * r + 8, 128 * w : 128 * w + 128] = large[r][w]

    def keep_f(c, slot, value):
        u1f[c, slot] = value

    def keep_c(c, slot, value):
        u1c[c, slot] = value

    def out_f(c, slot, value):
        fine_out[c, slot - 1] = value

    def out_c(c, slot, value):
        coarse_out[c, slot - 1] = value

    first_f = Step(FL, qf, qf, lambda c, s: qf[6 + c, s], 9, True, keep_f, (0, 0))
    first_c = Step(CL, qc, qc, lambda c, s: qc[5 + c, s], 8, False, keep_c, (0, 0))
    second_f = Step(FL, u1f, qf, lambda c, s: qf[c, s], 9, True, out_f, (8, 128))
    second_c = Step(CL, u1c, qc, lambda c, s: qc[c, s], 8, False, out_c, (8, 128))

    first_f.inner()
    first_c.inner()

    @pl.when(top)
    def _():
        for part in from_bottom:
            for copy in part:
                copy.wait_recv()

    @pl.when(jnp.logical_not(top))
    def _():
        for part in from_top:
            for copy in part:
                copy.wait_recv()
        prolonged(0, qf)

    mine_f, theirs_f = jnp.where(top, FL, 1), jnp.where(top, 0, FL + 1)
    mine_c, theirs_c = jnp.where(top, CL, 1), jnp.where(top, 0, CL + 1)
    later_f = deep_copy(u1f.at[pl.ds(0, 3), mine_f], u1f.at[pl.ds(0, 3), theirs_f], 1, 0)
    later_c = deep_copy(u1c.at[pl.ds(0, 3), mine_c], u1c.at[pl.ds(0, 3), theirs_c], 1, 1)
    down = deep_copy(u1c.at[pl.ds(0, 3), 1], got.at[1], 1, 2)
    up = deep_copy(give.at[1], u1c.at[pl.ds(0, 3), 0], 1, 2)

    first_f.outer()
    later_f.start()
    restricted(1, u1f, ((0, 0), (0, 1), (1, 0), (1, 1)))

    @pl.when(jnp.logical_not(top))
    def _():
        up.start()

    first_c.outer()
    later_c.start()

    @pl.when(top)
    def _():
        down.start()

    second_f.inner()
    second_c.inner()
    later_f.wait_recv()
    later_c.wait_recv()

    @pl.when(top)
    def _():
        up.wait_recv()

    @pl.when(jnp.logical_not(top))
    def _():
        down.wait_recv()
        prolonged(1, u1f)

    second_f.outer()
    second_c.outer()

    later_f.wait_send()
    later_c.wait_send()

    @pl.when(top)
    def _():
        for copy in [copy for part in from_top for copy in part] + [down]:
            copy.wait_send()

    @pl.when(jnp.logical_not(top))
    def _():
        for copy in [copy for part in from_bottom for copy in part] + [up]:
            copy.wait_send()

    for k, copy in sends:
        @pl.when(there[k][1])
        def _(copy=copy):
            copy.wait_send()


def store(fine, coarse, fine_out, coarse_out, sems):
    copies = [pltpu.make_async_copy(fine, fine_out, sems.at[0]), pltpu.make_async_copy(coarse, coarse_out, sems.at[1])]
    for copy in copies:
        copy.start()
    for copy in copies:
        copy.wait()


def per_device(*arrays):
    fine, coarse = arrays[0], arrays[3]
    after = stepped(arrays, fine, coarse)
    return pl.pallas_call(
        store,
        out_shape=(jax.ShapeDtypeStruct(fine.shape, F32), jax.ShapeDtypeStruct(coarse.shape, F32)),
        in_specs=[pl.BlockSpec(memory_space=pltpu.VMEM)] * 2,
        out_specs=(pl.BlockSpec(memory_space=pltpu.HBM), pl.BlockSpec(memory_space=pltpu.HBM)),
        scratch_shapes=[pltpu.SemaphoreType.DMA((2,))],
    )(*[pltpu.with_memory_space_constraint(a, pltpu.VMEM) for a in after])


def stepped(arrays, fine, coarse):
    return pl.pallas_call(
        kernel,
        out_shape=(pltpu.VMEM(fine.shape, F32), pltpu.VMEM(coarse.shape, F32)),
        in_specs=[pl.BlockSpec(memory_space=pltpu.HBM)] * 6,
        out_specs=(pl.BlockSpec(memory_space=pltpu.VMEM), pl.BlockSpec(memory_space=pltpu.VMEM)),
        scratch_shapes=[
            pltpu.VMEM((FQ, FL + 2, FR, FW), F32),
            pltpu.VMEM((CQ, CL + 2, CR, CW), F32),
            pltpu.VMEM((3, FL + 2, FR, FW), F32),
            pltpu.VMEM((3, CL + 2, CR, CW), F32),
            pltpu.VMEM((X_LOW_ROWS, 128), F32),
            pltpu.VMEM((X_ROWS, 128), F32),
            pltpu.VMEM((Y_ROWS + C_FINE, 128), F32),
            pltpu.VMEM((X_LOW_ROWS, 128), F32),
            pltpu.VMEM((X_ROWS, 128), F32),
            pltpu.VMEM((2, Y_ROWS, 128), F32),
            pltpu.VMEM((4, C_ROWS, 128), F32),
            pltpu.VMEM((STEPS, 3, CR, CW), F32),
            pltpu.VMEM((STEPS, 3, CR, CW), F32),
            pltpu.SemaphoreType.DMA((8,)),
            pltpu.SemaphoreType.DMA((10,)),
            pltpu.SemaphoreType.DMA((10,)),
            pltpu.SemaphoreType.DMA((STEPS, 9)),
            pltpu.SemaphoreType.DMA((STEPS, 9)),
        ],
        compiler_params=pltpu.CompilerParams(
            collective_id=0, has_side_effects=True, vmem_limit_bytes=40 * 2**20
        ),
    )(*[pltpu.with_memory_space_constraint(a, pltpu.HBM) for a in arrays])


def solution(mesh):
    spec = P(None, "dev", "gx", "gy")
    return jax.shard_map(
        per_device, mesh=mesh, in_specs=(spec,) * 6, out_specs=(spec, spec), check_vma=False
    )
```

```python
import jax
import jax.numpy as jnp
from jax import lax
from jax.experimental import pallas as pl
from jax.experimental.pallas import tpu as pltpu
from jax.sharding import PartitionSpec as P

STEPS = 2
STEP_SQUARED = 0.15 * 0.15
MESH = pl.DeviceIdType.MESH
F32 = jnp.float32

FR, FW = 24, 384
CR, CW = 16, 256
FL, CL = 4, 8
FQ = 10
CQ = 9

X_COARSE = 6 * 16
X_EXTRA = X_COARSE + 10 * 8
X_LOW_FIRST = X_EXTRA
X_HIGH_FIRST = X_EXTRA + 2 * 16
X_REST = 4 * 16 + 4 * 8
X_LOW_ROWS = X_LOW_FIRST + X_REST
X_ROWS = X_HIGH_FIRST + X_REST
Y_FINE = 32
Y_COARSE = 24
Y_ROWS = Y_FINE + Y_COARSE
C_ROWS = 16
SIDES = ((-1, 0), (1, 0), (0, -1), (0, 1), (-1, -1), (-1, 1), (1, -1), (1, 1))


def iota(shape, dim):
    return lax.broadcasted_iota(jnp.int32, shape, dim)


def turned(value, shift, axis):
    shift = shift % value.shape[axis]
    return pltpu.roll(value, shift, axis) if shift else value


def picked(tile, index, axis):
    return jnp.take_along_axis(tile, index, axis=axis)


def restrict(tiles, r, w):
    row, lane = iota((8, 128), 0), iota((8, 128), 1)
    row_at, lane_at = (2 * row) & 7, (2 * lane) & 127

    def pairs(tile, axis, at):
        return picked(tile + turned(tile, -1, axis), at, axis)

    def joined(values, half, at):
        return values[0] if len(values) == 1 else jnp.where(at < half, values[0], values[1])

    sources = ((0,), (1, 2))
    columns = [joined([pairs(tiles(a, b), 0, row_at) for a in sources[r]], 4, row) for b in sources[w]]
    return joined([0.25 * pairs(v, 1, lane_at) for v in columns], 64, lane)


def prolong(tiles):
    row, lane = iota((8, 128), 0), iota((8, 128), 1)

    def spread(halo, own, half, at, axis):
        low = at // 2
        return (
            picked(halo, jnp.where(at < half, low, low + half), axis),
            picked(own, low, axis),
            picked(own, low + half, axis),
        )

    rows = [spread(tiles(r, 0), tiles(r, 1), 64, lane, 1) for r in range(2)]
    columns = [spread(rows[0][w], rows[1][w], 4, row, 0) for w in range(3)]
    return [[columns[w][r] for w in range(3)] for r in range(3)]


def gradients_to_stress(here, below, medium, stretch, which):
    def ahead(value, axis):
        return turned(value, -1, axis)

    mu, lam = medium
    dz = [b - h for b, h in zip(below, here)]
    if stretch is not None:
        dz = [d * stretch for d in dz]
    dx = [ahead(h, 0) - h for h in here]
    dy = [ahead(h, 1) - h for h in here]
    bulk = lam * (dx[0] + dy[1] + dz[2])
    twice = mu + mu
    out = {"zz": bulk + twice * dz[2], "xz": mu * (dz[0] + dx[2]), "yz": mu * (dz[1] + dy[2])}
    if which == "all":
        out["xx"] = bulk + twice * dx[0]
        out["yy"] = bulk + twice * dy[1]
        out["xy"] = mu * (dy[0] + dx[1])
    return out


class Step:
    def __init__(self, count, cur, qty, before_at, scale_at, stretched, write, crop):
        self.count, self.cur, self.qty, self.before_at = count, cur, qty, before_at
        self.scale_at, self.stretched, self.write, self.crop = scale_at, stretched, write, crop

    def cut(self, value):
        return value[self.crop[0] :, self.crop[1] :]

    def stress(self, slot, which="all"):
        cur, qty = self.cur, self.qty
        stretch = qty[5, slot] if self.stretched else None
        return gradients_to_stress(
            [cur[c, slot] for c in range(3)],
            [cur[c, slot + 1] for c in range(3)],
            (qty[3, slot], qty[4, slot]),
            stretch,
            which,
        )

    def move(self, slot, s, above):
        cut = self.cut

        def back_x(name):
            return cut(s[name]) - cut(turned(s[name], 1, 0))

        def back_y(name):
            return cut(s[name]) - cut(turned(s[name], 1, 1))

        def back_z(name):
            d = cut(s[name]) - cut(above[name])
            return d * cut(self.qty[5, slot]) if self.stretched else d

        force = (
            back_x("xx") + back_y("xy") + back_z("xz"),
            back_x("xy") + back_y("yy") + back_z("yz"),
            back_x("xz") + back_y("yz") + back_z("zz"),
        )
        scale = cut(self.qty[self.scale_at, slot])
        for c in range(3):
            now = cut(self.cur[c, slot])
            before = cut(self.before_at(c, slot))
            self.write(c, slot, now + now - before + scale * force[c])

    def inner(self):
        self.first = above = self.stress(1)
        for slot in range(2, self.count):
            s = self.stress(slot)
            self.move(slot, s, above)
            above = s
        self.above = above

    def outer(self):
        last = self.stress(self.count)
        self.move(self.count, last, self.above)
        self.move(1, self.first, self.stress(0, "vertical"))


def fine_at(g, first):
    return g * 16 if g < 6 else first + (g - 6) * 16


def pack_x(qf, qc, low, high):
    row8 = iota((8, 256), 0)
    crow = iota((8, 128), 0)

    def store(ref, at, value):
        ref[pl.ds(at, 8), :] = value[:, :128]
        ref[pl.ds(at + 8, 8), :] = value[:, 128:]

    for g in range(FQ):
        up = jnp.zeros((8, 256), F32)
        down = up
        for l in range(FL):
            z = jnp.where(row8 < 4, qf[g, l + 1, 8:16, 128:], qf[g, l + 1, 16:24, 128:])
            t = turned(z, 2 * l, 0)
            up = t if l == 0 else jnp.where(row8 // 2 == l, t, up)
            down = t if l == 0 else jnp.where(row8 // 2 == l - 1, t, down)
        store(high, fine_at(g, X_HIGH_FIRST), up)
        store(low, fine_at(g, X_LOW_FIRST), down)
    for q in range(5):
        for half in range(2):
            for l in range(4):
                t = turned(qc[q, half * 4 + l + 1, 8:16, 128:], 2 * l, 0)
                up = t if l == 0 else jnp.where(crow // 2 == l, t, up)
                down = t if l == 0 else jnp.where(crow // 2 == l - 1, t, down)
            at = X_COARSE + (q * 2 + half) * 8
            high[pl.ds(at, 8), :] = up
            low[pl.ds(at, 8), :] = down
    for q in range(4):
        for l in range(8):
            t = turned(qc[5 + q, l + 1, 8:16, 128:], l, 0)
            up = t if l == 0 else jnp.where(crow == l, t, up)
            down = t if l == 0 else jnp.where(crow == l - 1, t, down)
        high[pl.ds(X_HIGH_FIRST + 64 + q * 8, 8), :] = up
        low[pl.ds(X_LOW_FIRST + 64 + q * 8, 8), :] = down
    more = [jnp.where(row8 < 2, turned(qf[c, 3, 8:16, 128:], -2, 0), qf[c, 4, 8:16, 128:]) for c in range(3)]
    store(high, X_EXTRA, jnp.where(row8 < 4, more[0], turned(more[1], 4, 0)))
    store(high, X_EXTRA + 16, more[2])


def unpack_x(qf, qc, low, high, first):
    row8 = iota((8, 256), 0)
    crow = iota((8, 128), 0)

    def load(ref, at):
        return jnp.concatenate([ref[pl.ds(at, 8), :], ref[pl.ds(at + 8, 8), :]], axis=1)

    for g in range(6) if first else range(6, FQ):
        up = load(high, fine_at(g, X_HIGH_FIRST))
        down = load(low, fine_at(g, X_LOW_FIRST))
        more = turned(load(high, X_EXTRA + g // 2 * 16), -4 * (g % 2), 0) if g < 3 else None
        for l in range(FL):
            t = jnp.where(row8 < 4, turned(up, -2 * l, 0), turned(down, -2 * l, 0))
            if g < 3 and l == 2:
                t = jnp.where(row8 // 2 == 1, turned(more, 2, 0), t)
            if g < 3 and l == 3:
                t = jnp.where(row8 // 2 == 1, more, t)
            qf[g, l + 1, 0:8, 128:] = t
    for q in range(5) if first else ():
        for half in range(2):
            at = X_COARSE + (q * 2 + half) * 8
            up = high[pl.ds(at, 8), :]
            down = low[pl.ds(at, 8), :]
            for l in range(4):
                t = jnp.where(crow < 4, turned(up, -2 * l, 0), turned(down, -2 * l, 0))
                qc[q, half * 4 + l + 1, 0:8, 128:] = t
    for q in () if first else range(4):
        up = high[pl.ds(X_HIGH_FIRST + 64 + q * 8, 8), :]
        down = low[pl.ds(X_LOW_FIRST + 64 + q * 8, 8), :]
        for l in range(8):
            qc[5 + q, l + 1, 0:8, 128:] = jnp.where(crow < 4, turned(up, -l, 0), turned(down, -l, 0))


def pack_y(qf, qc, out, corner):
    lane = iota((16, 128), 1)
    lane8 = iota((8, 128), 1)
    row8 = iota((8, 128), 0)
    fine, coarse = [], []
    for t in range(2):
        packed = jnp.zeros((16, 128), F32)
        for k in range(20):
            g, l = t * 5 + k // 4, k % 4
            z = jnp.where(lane < 64, qf[g, l + 1, 8:24, 128:256], qf[g, l + 1, 8:24, 256:384])
            mine = ((lane + (2 - 6 * k + 128)) & 127) < 6
            packed = jnp.where(mine, turned(z, 6 * k, 1), packed)
        out[pl.ds(t * 16, 16), :] = packed
        fine.append(packed)
    for t in range(3):
        packed = jnp.zeros((8, 128), F32)
        for k in range(32 if t < 2 else 8):
            q, l = t * 4 + k // 8, k % 8
            mine = ((lane8 + (2 - 4 * k + 128)) & 127) < 4
            packed = jnp.where(mine, turned(qc[q, l + 1, 8:16, 128:256], 4 * k, 1), packed)
        out[pl.ds(Y_FINE + t * 8, 8), :] = packed
        coarse.append(packed)
    corner[0, 0:8] = jnp.where(row8 < 4, fine[0][:8], turned(fine[1][:8], 4, 0))
    corner[0, 8:16] = jnp.where(
        row8 < 2, coarse[0], jnp.where(row8 < 4, turned(coarse[1], 2, 0), turned(coarse[2], 4, 0))
    )
    corner[1, 0:8] = jnp.where(row8 >= 6, fine[0][8:], turned(fine[1][8:], -2, 0))
    corner[1, 8:16] = jnp.where(
        row8 >= 6, coarse[0], jnp.where(row8 >= 4, turned(coarse[1], -2, 0), turned(coarse[2], -4, 0))
    )


def unpack_y(qf, qc, side, corner):
    lane = iota((16, 128), 1)
    lane8 = iota((8, 128), 1)
    row8 = iota((8, 128), 0)
    fine_low = ((lane + 2) & 127) % 6 < 2
    fine_low8 = ((lane8 + 2) & 127) % 6 < 2
    coarse_low8 = ((lane8 + 2) & 127) % 4 < 2

    def corners(at, low, up, down):
        before = jnp.where(low, corner[0, at : at + 8], corner[1, at : at + 8])
        after = jnp.where(low, corner[2, at : at + 8], corner[3, at : at + 8])
        return jnp.where(row8 < 4, turned(after, up, 0), turned(before, down, 0))

    for t in range(2):
        own = jnp.where(fine_low, side[0, pl.ds(t * 16, 16), :], side[1, pl.ds(t * 16, 16), :])
        both = jnp.concatenate([corners(0, fine_low8, -4 * t, 2 * t), own], axis=0)
        for k in range(20):
            g, l = t * 5 + k // 4, k % 4
            qf[g, l + 1, :, 0:128] = turned(both, -6 * k, 1)
    for t in range(3):
        at = Y_FINE + t * 8
        own = jnp.where(coarse_low8, side[0, pl.ds(at, 8), :], side[1, pl.ds(at, 8), :])
        both = jnp.concatenate([corners(8, coarse_low8, -2 * t, 2 * t), own], axis=0)
        for k in range(32 if t < 2 else 8):
            q, l = t * 4 + k // 8, k % 8
            qc[q, l + 1, :, 0:128] = turned(both, -4 * k, 1)


def kernel(
    fine_now, fine_before, fine_material, coarse_now, coarse_before, coarse_material,
    fine_out, coarse_out,
    qf, qc, u1f, u1c,
    sx_low, sx_high, sy, sc, rx_low, rx_high, ry, rc,
    give, got,
    load_sem, send_sem, recv_sem, deep_send, deep_recv,
):
    gx, gy, dev = lax.axis_index("gx"), lax.axis_index("gy"), lax.axis_index("dev")
    nx, ny = lax.axis_size("gx"), lax.axis_size("gy")
    top = dev == 0
    partner = {"gx": gx, "gy": gy, "dev": 1 - dev}
    there = []
    for dx, dy in SIDES:
        x, y = gx + dx, gy + dy
        there.append(({"gx": x, "gy": y, "dev": dev}, (x >= 0) & (x < nx) & (y >= 0) & (y < ny)))

    barrier = pltpu.get_barrier_semaphore()
    expected = 1
    pl.semaphore_signal(barrier, inc=1, device_id=partner, device_id_type=MESH)
    for where, present in there:
        @pl.when(present)
        def _(where=where):
            pl.semaphore_signal(barrier, inc=1, device_id=where, device_id_type=MESH)
        expected = expected + jnp.where(present, 1, 0)

    fine_own = (pl.ds(1, FL), pl.ds(8, 16), pl.ds(128, 256))
    coarse_own = (pl.ds(1, CL), pl.ds(8, 8), pl.ds(128, 128))
    loads = [
        (fine_now, qf.at[(pl.ds(0, 3), *fine_own)]),
        (fine_material.at[pl.ds(1, 3)], qf.at[(pl.ds(3, 3), *fine_own)]),
        (fine_before, qf.at[(pl.ds(6, 3), *fine_own)]),
        (fine_material.at[pl.ds(0, 1)], qf.at[(pl.ds(9, 1), *fine_own)]),
        (coarse_now, qc.at[(pl.ds(0, 3), *coarse_own)]),
        (coarse_material.at[pl.ds(1, 2)], qc.at[(pl.ds(3, 2), *coarse_own)]),
        (coarse_before, qc.at[(pl.ds(5, 3), *coarse_own)]),
        (coarse_material.at[pl.ds(0, 1)], qc.at[(pl.ds(8, 1), *coarse_own)]),
    ]
    copies = [pltpu.make_async_copy(src, dst, load_sem.at[k]) for k, (src, dst) in enumerate(loads)]
    for copy in copies:
        copy.start()

    def zero_unless(present, ref, at=None):
        @pl.when(jnp.logical_not(present))
        def _():
            if at is None:
                ref[...] = jnp.zeros(ref.shape, F32)
            else:
                ref[at] = jnp.zeros(ref.shape[1:], F32)

    zero_unless(there[0][1], rx_low)
    zero_unless(there[1][1], rx_high)
    for k in range(2):
        zero_unless(there[2 + k][1], ry, k)
    for k in range(4):
        zero_unless(there[4 + k][1], rc, k)

    @pl.when(top)
    def _():
        for c in range(3):
            qf[c, 0] = jnp.zeros((FR, FW), F32)
            u1f[c, 0] = jnp.zeros((FR, FW), F32)
        for k in range(3, 6):
            qf[k, 0] = jnp.zeros((FR, FW), F32)

    @pl.when(jnp.logical_not(top))
    def _():
        for c in range(3):
            qc[c, CL + 1] = jnp.zeros((CR, CW), F32)
            u1c[c, CL + 1] = jnp.zeros((CR, CW), F32)

    for copy in copies:
        copy.wait()
    for l in range(FL):
        own = (9, l + 1, pl.ds(8, 16), pl.ds(128, 256))
        qf[own] = STEP_SQUARED / qf[own]
    for l in range(CL):
        own = (8, l + 1, pl.ds(8, 8), pl.ds(128, 128))
        qc[own] = (0.25 * STEP_SQUARED) / qc[own]
    pack_x(qf, qc, sx_low, sx_high)
    pack_y(qf, qc, sy, sc)

    areas = (
        ((pl.ds(8, 16), pl.ds(128, 256)), (pl.ds(8, 8), pl.ds(128, 128)), ((1, 1),)),
        ((pl.ds(0, FR), pl.ds(0, 128)), (pl.ds(0, CR), pl.ds(0, 128)), ((0, 0), (1, 0))),
        ((pl.ds(0, 8), pl.ds(128, 256)), (pl.ds(0, 8), pl.ds(128, 128)), ((0, 1),)),
    )

    def deep_copy(src, dst, phase, k):
        return pltpu.make_async_remote_copy(
            src, dst, deep_send.at[phase, k], deep_recv.at[phase, k], device_id=partner, device_id_type=MESH
        )

    def restricted(phase, cur_f, places):
        @pl.when(jnp.logical_not(top))
        def _():
            for c in range(3):
                for r, w in places:
                    give[phase, c, 8 * r : 8 * r + 8, 128 * w : 128 * w + 128] = restrict(
                        lambda a, b: cur_f[c, FL, 8 * a : 8 * a + 8, 128 * b : 128 * b + 128], r, w
                    )

    from_top, from_bottom = [], []
    for part, (fine, coarse, _) in enumerate(areas):
        from_top.append(
            [
                deep_copy(qf.at[(pl.ds(0, 6), FL, *fine)], qf.at[(pl.ds(0, 6), 0, *fine)], 0, part * 3),
                deep_copy(qc.at[(pl.ds(0, 5), CL, *coarse)], qc.at[(pl.ds(0, 5), 0, *coarse)], 0, part * 3 + 1),
                deep_copy(qc.at[(pl.ds(0, 3), 1, *coarse)], got.at[(0, pl.ds(0, 3), *coarse)], 0, part * 3 + 2),
            ]
        )
        from_bottom.append(
            [
                deep_copy(qf.at[(pl.ds(0, 3), 1, *fine)], qf.at[(pl.ds(0, 3), FL + 1, *fine)], 0, part * 3),
                deep_copy(qc.at[(pl.ds(0, 3), 1, *coarse)], qc.at[(pl.ds(0, 3), CL + 1, *coarse)], 0, part * 3 + 1),
                deep_copy(give.at[(0, pl.ds(0, 3), *coarse)], qc.at[(pl.ds(0, 3), 0, *coarse)], 0, part * 3 + 2),
            ]
        )

    def start_part(part):
        @pl.when(top)
        def _():
            for copy in from_top[part]:
                copy.start()

        @pl.when(jnp.logical_not(top))
        def _():
            for copy in from_bottom[part]:
                copy.start()

    restricted(0, qf, areas[0][2])
    pl.semaphore_wait(barrier, expected)

    high_first, high_rest = pl.ds(0, X_HIGH_FIRST), pl.ds(X_HIGH_FIRST, X_REST)
    low_first, low_rest = pl.ds(0, X_LOW_FIRST), pl.ds(X_LOW_FIRST, X_REST)
    messages = [
        (0, sx_high.at[high_first], rx_high.at[high_first]), (1, sx_low.at[low_first], rx_low.at[low_first]),
        (2, sy, ry.at[1]), (3, sy, ry.at[0]),
        (4, sc.at[0], rc.at[3]), (5, sc.at[0], rc.at[2]), (6, sc.at[1], rc.at[1]), (7, sc.at[1], rc.at[0]),
        (0, sx_high.at[high_rest], rx_high.at[high_rest]), (1, sx_low.at[low_rest], rx_low.at[low_rest]),
    ]
    sends = []
    for n, (k, src, dst) in enumerate(messages):
        copy = pltpu.make_async_remote_copy(
            src, dst, send_sem.at[n], recv_sem.at[n], device_id=there[k][0], device_id_type=MESH
        )

        @pl.when(there[k][1])
        def _(copy=copy):
            copy.start()

        sends.append((k, copy))

    def arrived(*numbers):
        for n in numbers:
            k, copy = sends[n]
            opposite = SIDES.index((-SIDES[k][0], -SIDES[k][1]))

            @pl.when(there[opposite][1])
            def _(copy=copy):
                copy.wait_recv()

    start_part(0)
    arrived(2, 3, 4, 5, 6, 7)
    unpack_y(qf, qc, ry, rc)
    restricted(0, qf, areas[1][2])
    start_part(1)
    arrived(0, 1)
    unpack_x(qf, qc, rx_low, rx_high, True)
    restricted(0, qf, areas[2][2])
    start_part(2)

    @pl.when(top)
    def _():
        for k in range(3, 5):
            qc[k, 0] = qc[k, 1]

    arrived(8, 9)
    unpack_x(qf, qc, rx_low, rx_high, False)

    def prolonged(phase, cur_f):
        for c in range(3):
            large = prolong(lambda r, w: got[phase, c, 8 * r : 8 * r + 8, 128 * w : 128 * w + 128])
            for r in range(3):
                for w in range(3):
                    cur_f[c, FL + 1, 8 * r : 8 * r + 8, 128 * w : 128 * w + 128] = large[r][w]

    def keep_f(c, slot, value):
        u1f[c, slot] = value

    def keep_c(c, slot, value):
        u1c[c, slot] = value

    def out_f(c, slot, value):
        fine_out[c, slot - 1] = value

    def out_c(c, slot, value):
        coarse_out[c, slot - 1] = value

    first_f = Step(FL, qf, qf, lambda c, s: qf[6 + c, s], 9, True, keep_f, (0, 0))
    first_c = Step(CL, qc, qc, lambda c, s: qc[5 + c, s], 8, False, keep_c, (0, 0))
    second_f = Step(FL, u1f, qf, lambda c, s: qf[c, s], 9, True, out_f, (8, 128))
    second_c = Step(CL, u1c, qc, lambda c, s: qc[c, s], 8, False, out_c, (8, 128))

    first_f.inner()
    first_c.inner()

    @pl.when(top)
    def _():
        for part in from_bottom:
            for copy in part:
                copy.wait_recv()

    @pl.when(jnp.logical_not(top))
    def _():
        for part in from_top:
            for copy in part:
                copy.wait_recv()
        prolonged(0, qf)

    mine_f, theirs_f = jnp.where(top, FL, 1), jnp.where(top, 0, FL + 1)
    mine_c, theirs_c = jnp.where(top, CL, 1), jnp.where(top, 0, CL + 1)
    later_f = deep_copy(u1f.at[pl.ds(0, 3), mine_f], u1f.at[pl.ds(0, 3), theirs_f], 1, 0)
    later_c = deep_copy(u1c.at[pl.ds(0, 3), mine_c], u1c.at[pl.ds(0, 3), theirs_c], 1, 1)
    down = deep_copy(u1c.at[pl.ds(0, 3), 1], got.at[1], 1, 2)
    up = deep_copy(give.at[1], u1c.at[pl.ds(0, 3), 0], 1, 2)

    first_f.outer()
    later_f.start()
    restricted(1, u1f, ((0, 0), (0, 1), (1, 0), (1, 1)))

    @pl.when(jnp.logical_not(top))
    def _():
        up.start()

    first_c.outer()
    later_c.start()

    @pl.when(top)
    def _():
        down.start()

    second_f.inner()
    second_c.inner()
    later_f.wait_recv()
    later_c.wait_recv()

    @pl.when(top)
    def _():
        up.wait_recv()

    @pl.when(jnp.logical_not(top))
    def _():
        down.wait_recv()
        prolonged(1, u1f)

    second_f.outer()
    second_c.outer()

    later_f.wait_send()
    later_c.wait_send()

    @pl.when(top)
    def _():
        for copy in [copy for part in from_top for copy in part] + [down]:
            copy.wait_send()

    @pl.when(jnp.logical_not(top))
    def _():
        for copy in [copy for part in from_bottom for copy in part] + [up]:
            copy.wait_send()

    for k, copy in sends:
        @pl.when(there[k][1])
        def _(copy=copy):
            copy.wait_send()


def store(fine, coarse, fine_out, coarse_out, sems):
    copies = [pltpu.make_async_copy(fine, fine_out, sems.at[0]), pltpu.make_async_copy(coarse, coarse_out, sems.at[1])]
    for copy in copies:
        copy.start()
    for copy in copies:
        copy.wait()


def per_device(*arrays):
    fine, coarse = arrays[0], arrays[3]
    after = stepped(arrays, fine, coarse)
    return pl.pallas_call(
        store,
        out_shape=(jax.ShapeDtypeStruct(fine.shape, F32), jax.ShapeDtypeStruct(coarse.shape, F32)),
        in_specs=[pl.BlockSpec(memory_space=pltpu.VMEM)] * 2,
        out_specs=(pl.BlockSpec(memory_space=pltpu.HBM), pl.BlockSpec(memory_space=pltpu.HBM)),
        scratch_shapes=[pltpu.SemaphoreType.DMA((2,))],
    )(*[pltpu.with_memory_space_constraint(a, pltpu.VMEM) for a in after])


def stepped(arrays, fine, coarse):
    return pl.pallas_call(
        kernel,
        out_shape=(pltpu.VMEM(fine.shape, F32), pltpu.VMEM(coarse.shape, F32)),
        in_specs=[pl.BlockSpec(memory_space=pltpu.HBM)] * 6,
        out_specs=(pl.BlockSpec(memory_space=pltpu.VMEM), pl.BlockSpec(memory_space=pltpu.VMEM)),
        scratch_shapes=[
            pltpu.VMEM((FQ, FL + 2, FR, FW), F32),
            pltpu.VMEM((CQ, CL + 2, CR, CW), F32),
            pltpu.VMEM((3, FL + 2, FR, FW), F32),
            pltpu.VMEM((3, CL + 2, CR, CW), F32),
            pltpu.VMEM((X_LOW_ROWS, 128), F32),
            pltpu.VMEM((X_ROWS, 128), F32),
            pltpu.VMEM((Y_ROWS, 128), F32),
            pltpu.VMEM((2, C_ROWS, 128), F32),
            pltpu.VMEM((X_LOW_ROWS, 128), F32),
            pltpu.VMEM((X_ROWS, 128), F32),
            pltpu.VMEM((2, Y_ROWS, 128), F32),
            pltpu.VMEM((4, C_ROWS, 128), F32),
            pltpu.VMEM((STEPS, 3, CR, CW), F32),
            pltpu.VMEM((STEPS, 3, CR, CW), F32),
            pltpu.SemaphoreType.DMA((8,)),
            pltpu.SemaphoreType.DMA((10,)),
            pltpu.SemaphoreType.DMA((10,)),
            pltpu.SemaphoreType.DMA((STEPS, 9)),
            pltpu.SemaphoreType.DMA((STEPS, 9)),
        ],
        compiler_params=pltpu.CompilerParams(
            collective_id=0, has_side_effects=True, vmem_limit_bytes=40 * 2**20
        ),
    )(*[pltpu.with_memory_space_constraint(a, pltpu.HBM) for a in arrays])


def solution(mesh):
    spec = P(None, "dev", "gx", "gy")
    return jax.shard_map(
        per_device, mesh=mesh, in_specs=(spec,) * 6, out_specs=(spec, spec), check_vma=False
    )
```

```python
import jax
import jax.numpy as jnp
from jax import lax
from jax.experimental import pallas as pl
from jax.experimental.pallas import tpu as pltpu
from jax.sharding import PartitionSpec as P

STEPS = 2
STEP_SQUARED = 0.15 * 0.15
MESH = pl.DeviceIdType.MESH
F32 = jnp.float32

FR, FW = 24, 384
CR, CW = 16, 256
FL, CL = 4, 8
FQ = 10
CQ = 9

X_COARSE = 6 * 16
X_MEDIUM = X_COARSE + 6 * 8
X_EXTRA = X_MEDIUM + 2 * 8
X_LOW_FIRST = X_COARSE + 10 * 8
X_HIGH_FIRST = X_EXTRA + 2 * 16
X_REST = 4 * 16 + 4 * 8
X_LOW_ROWS = X_LOW_FIRST + X_REST
X_ROWS = X_HIGH_FIRST + X_REST
Y_FINE = 32
Y_COARSE = 24
Y_ROWS = Y_FINE + Y_COARSE
C_ROWS = 16
SIDES = ((-1, 0), (1, 0), (0, -1), (0, 1), (-1, -1), (-1, 1), (1, -1), (1, 1))


def iota(shape, dim):
    return lax.broadcasted_iota(jnp.int32, shape, dim)


def turned(value, shift, axis):
    shift = shift % value.shape[axis]
    return pltpu.roll(value, shift, axis) if shift else value


def picked(tile, index, axis):
    return jnp.take_along_axis(tile, index, axis=axis)


def restrict(tiles, r, w):
    row, lane = iota((8, 128), 0), iota((8, 128), 1)
    row_at, lane_at = (2 * row) & 7, (2 * lane) & 127

    def pairs(tile, axis, at):
        return picked(tile + turned(tile, -1, axis), at, axis)

    def joined(values, half, at):
        return values[0] if len(values) == 1 else jnp.where(at < half, values[0], values[1])

    sources = ((0,), (1, 2))
    columns = [joined([pairs(tiles(a, b), 0, row_at) for a in sources[r]], 4, row) for b in sources[w]]
    return joined([0.25 * pairs(v, 1, lane_at) for v in columns], 64, lane)


def prolong(tiles):
    row, lane = iota((8, 128), 0), iota((8, 128), 1)

    def spread(halo, own, half, at, axis):
        low = at // 2
        return (
            picked(halo, jnp.where(at < half, low, low + half), axis),
            picked(own, low, axis),
            picked(own, low + half, axis),
        )

    rows = [spread(tiles(r, 0), tiles(r, 1), 64, lane, 1) for r in range(2)]
    columns = [spread(rows[0][w], rows[1][w], 4, row, 0) for w in range(3)]
    return [[columns[w][r] for w in range(3)] for r in range(3)]


def gradients_to_stress(here, below, medium, stretch, which):
    def ahead(value, axis):
        return turned(value, -1, axis)

    mu, lam = medium
    dz = [b - h for b, h in zip(below, here)]
    if stretch is not None:
        dz = [d * stretch for d in dz]
    dx = [ahead(h, 0) - h for h in here]
    dy = [ahead(h, 1) - h for h in here]
    bulk = lam * (dx[0] + dy[1] + dz[2])
    twice = mu + mu
    out = {"zz": bulk + twice * dz[2], "xz": mu * (dz[0] + dx[2]), "yz": mu * (dz[1] + dy[2])}
    if which == "all":
        out["xx"] = bulk + twice * dx[0]
        out["yy"] = bulk + twice * dy[1]
        out["xy"] = mu * (dy[0] + dx[1])
    return out


class Step:
    def __init__(self, count, cur, qty, before_at, scale_at, stretched, write, crop):
        self.count, self.cur, self.qty, self.before_at = count, cur, qty, before_at
        self.scale_at, self.stretched, self.write, self.crop = scale_at, stretched, write, crop

    def cut(self, value):
        return value[self.crop[0] :, self.crop[1] :]

    def stress(self, slot, which="all"):
        cur, qty = self.cur, self.qty
        stretch = qty[5, slot] if self.stretched else None
        return gradients_to_stress(
            [cur[c, slot] for c in range(3)],
            [cur[c, slot + 1] for c in range(3)],
            (qty[3, slot], qty[4, slot]),
            stretch,
            which,
        )

    def move(self, slot, s, above):
        cut = self.cut

        def back_x(name):
            return cut(s[name]) - cut(turned(s[name], 1, 0))

        def back_y(name):
            return cut(s[name]) - cut(turned(s[name], 1, 1))

        def back_z(name):
            d = cut(s[name]) - cut(above[name])
            return d * cut(self.qty[5, slot]) if self.stretched else d

        force = (
            back_x("xx") + back_y("xy") + back_z("xz"),
            back_x("xy") + back_y("yy") + back_z("yz"),
            back_x("xz") + back_y("yz") + back_z("zz"),
        )
        scale = cut(self.qty[self.scale_at, slot])
        for c in range(3):
            now = cut(self.cur[c, slot])
            before = cut(self.before_at(c, slot))
            self.write(c, slot, now + now - before + scale * force[c])

    def inner(self):
        self.first = above = self.stress(1)
        for slot in range(2, self.count):
            s = self.stress(slot)
            self.move(slot, s, above)
            above = s
        self.above = above

    def outer(self):
        last = self.stress(self.count)
        self.move(self.count, last, self.above)
        self.move(1, self.first, self.stress(0, "vertical"))


def fine_at(g, first):
    return g * 16 if g < 6 else first + (g - 6) * 16


def pack_x(qf, qc, low, high):
    row8 = iota((8, 256), 0)
    crow = iota((8, 128), 0)

    def store(ref, at, value):
        ref[pl.ds(at, 8), :] = value[:, :128]
        ref[pl.ds(at + 8, 8), :] = value[:, 128:]

    for g in range(FQ):
        up = jnp.zeros((8, 256), F32)
        down = up
        for l in range(FL):
            z = jnp.where(row8 < 4, qf[g, l + 1, 8:16, 128:], qf[g, l + 1, 16:24, 128:])
            t = turned(z, 2 * l, 0)
            up = t if l == 0 else jnp.where(row8 // 2 == l, t, up)
            down = t if l == 0 else jnp.where(row8 // 2 == l - 1, t, down)
        store(high, fine_at(g, X_HIGH_FIRST), up)
        store(low, fine_at(g, X_LOW_FIRST), down)
    for q in range(5):
        for half in range(2):
            for l in range(4):
                t = turned(qc[q, half * 4 + l + 1, 8:16, 128:], 2 * l, 0)
                up = t if l == 0 else jnp.where(crow // 2 == l, t, up)
                down = t if l == 0 else jnp.where(crow // 2 == l - 1, t, down)
            at = X_COARSE + (q * 2 + half) * 8
            if q < 3:
                high[pl.ds(at, 8), :] = up
            low[pl.ds(at, 8), :] = down
    for q in range(3, 5):
        for l in range(8):
            t = turned(qc[q, l + 1, 8:16, 128:], l, 0)
            up = t if l == 0 else jnp.where(crow == l, t, up)
        high[pl.ds(X_MEDIUM + (q - 3) * 8, 8), :] = up
    for q in range(4):
        for l in range(8):
            t = turned(qc[5 + q, l + 1, 8:16, 128:], l, 0)
            up = t if l == 0 else jnp.where(crow == l, t, up)
            down = t if l == 0 else jnp.where(crow == l - 1, t, down)
        high[pl.ds(X_HIGH_FIRST + 64 + q * 8, 8), :] = up
        low[pl.ds(X_LOW_FIRST + 64 + q * 8, 8), :] = down
    more = [jnp.where(row8 < 2, turned(qf[c, 3, 8:16, 128:], -2, 0), qf[c, 4, 8:16, 128:]) for c in range(3)]
    store(high, X_EXTRA, jnp.where(row8 < 4, more[0], turned(more[1], 4, 0)))
    store(high, X_EXTRA + 16, more[2])


def unpack_x(qf, qc, low, high, first):
    row8 = iota((8, 256), 0)
    crow = iota((8, 128), 0)

    def load(ref, at):
        return jnp.concatenate([ref[pl.ds(at, 8), :], ref[pl.ds(at + 8, 8), :]], axis=1)

    for g in range(6) if first else range(6, FQ):
        up = load(high, fine_at(g, X_HIGH_FIRST))
        down = load(low, fine_at(g, X_LOW_FIRST))
        more = turned(load(high, X_EXTRA + g // 2 * 16), -4 * (g % 2), 0) if g < 3 else None
        for l in range(FL):
            t = jnp.where(row8 < 4, turned(up, -2 * l, 0), turned(down, -2 * l, 0))
            if g < 3 and l == 2:
                t = jnp.where(row8 // 2 == 1, turned(more, 2, 0), t)
            if g < 3 and l == 3:
                t = jnp.where(row8 // 2 == 1, more, t)
            qf[g, l + 1, 0:8, 128:] = t
    for q in range(5) if first else ():
        for half in range(2):
            at = X_COARSE + (q * 2 + half) * 8
            up = high[pl.ds(at if q < 3 else X_MEDIUM + (q - 3) * 8, 8), :]
            down = low[pl.ds(at, 8), :]
            for l in range(4):
                shift = 2 * l if q < 3 else half * 4 + l
                t = jnp.where(crow < 4, turned(up, -shift, 0), turned(down, -2 * l, 0))
                qc[q, half * 4 + l + 1, 0:8, 128:] = t
    for q in () if first else range(4):
        up = high[pl.ds(X_HIGH_FIRST + 64 + q * 8, 8), :]
        down = low[pl.ds(X_LOW_FIRST + 64 + q * 8, 8), :]
        for l in range(8):
            qc[5 + q, l + 1, 0:8, 128:] = jnp.where(crow < 4, turned(up, -l, 0), turned(down, -l, 0))


def pack_y(qf, qc, out, corner):
    lane = iota((16, 128), 1)
    lane8 = iota((8, 128), 1)
    row8 = iota((8, 128), 0)
    fine, coarse = [], []
    for t in range(2):
        packed = jnp.zeros((16, 128), F32)
        for k in range(20):
            g, l = t * 5 + k // 4, k % 4
            z = jnp.where(lane < 64, qf[g, l + 1, 8:24, 128:256], qf[g, l + 1, 8:24, 256:384])
            mine = ((lane + (2 - 6 * k + 128)) & 127) < 6
            packed = jnp.where(mine, turned(z, 6 * k, 1), packed)
        out[pl.ds(t * 16, 16), :] = packed
        fine.append(packed)
    for t in range(3):
        packed = jnp.zeros((8, 128), F32)
        for k in range(32 if t < 2 else 8):
            q, l = t * 4 + k // 8, k % 8
            mine = ((lane8 + (2 - 4 * k + 128)) & 127) < 4
            packed = jnp.where(mine, turned(qc[q, l + 1, 8:16, 128:256], 4 * k, 1), packed)
        out[pl.ds(Y_FINE + t * 8, 8), :] = packed
        coarse.append(packed)
    corner[0, 0:8] = jnp.where(row8 < 4, fine[0][:8], turned(fine[1][:8], 4, 0))
    corner[0, 8:16] = jnp.where(
        row8 < 2, coarse[0], jnp.where(row8 < 4, turned(coarse[1], 2, 0), turned(coarse[2], 4, 0))
    )
    corner[1, 0:8] = jnp.where(row8 >= 6, fine[0][8:], turned(fine[1][8:], -2, 0))
    corner[1, 8:16] = jnp.where(
        row8 >= 6, coarse[0], jnp.where(row8 >= 4, turned(coarse[1], -2, 0), turned(coarse[2], -4, 0))
    )


def unpack_y(qf, qc, side, corner):
    lane = iota((16, 128), 1)
    lane8 = iota((8, 128), 1)
    row8 = iota((8, 128), 0)
    fine_low = ((lane + 2) & 127) % 6 < 2
    fine_low8 = ((lane8 + 2) & 127) % 6 < 2
    coarse_low8 = ((lane8 + 2) & 127) % 4 < 2

    def corners(at, low, up, down):
        before = jnp.where(low, corner[0, at : at + 8], corner[1, at : at + 8])
        after = jnp.where(low, corner[2, at : at + 8], corner[3, at : at + 8])
        return jnp.where(row8 < 4, turned(after, up, 0), turned(before, down, 0))

    for t in range(2):
        own = jnp.where(fine_low, side[0, pl.ds(t * 16, 16), :], side[1, pl.ds(t * 16, 16), :])
        both = jnp.concatenate([corners(0, fine_low8, -4 * t, 2 * t), own], axis=0)
        for k in range(20):
            g, l = t * 5 + k // 4, k % 4
            qf[g, l + 1, :, 0:128] = turned(both, -6 * k, 1)
    for t in range(3):
        at = Y_FINE + t * 8
        own = jnp.where(coarse_low8, side[0, pl.ds(at, 8), :], side[1, pl.ds(at, 8), :])
        both = jnp.concatenate([corners(8, coarse_low8, -2 * t, 2 * t), own], axis=0)
        for k in range(32 if t < 2 else 8):
            q, l = t * 4 + k // 8, k % 8
            qc[q, l + 1, :, 0:128] = turned(both, -4 * k, 1)


def kernel(
    fine_now, fine_before, fine_material, coarse_now, coarse_before, coarse_material,
    fine_out, coarse_out,
    qf, qc, u1f, u1c,
    sx_low, sx_high, sy, sc, rx_low, rx_high, ry, rc,
    give, got,
    load_sem, send_sem, recv_sem, deep_send, deep_recv,
):
    gx, gy, dev = lax.axis_index("gx"), lax.axis_index("gy"), lax.axis_index("dev")
    nx, ny = lax.axis_size("gx"), lax.axis_size("gy")
    top = dev == 0
    partner = {"gx": gx, "gy": gy, "dev": 1 - dev}
    there = []
    for dx, dy in SIDES:
        x, y = gx + dx, gy + dy
        there.append(({"gx": x, "gy": y, "dev": dev}, (x >= 0) & (x < nx) & (y >= 0) & (y < ny)))

    barrier = pltpu.get_barrier_semaphore()
    expected = 1
    pl.semaphore_signal(barrier, inc=1, device_id=partner, device_id_type=MESH)
    for where, present in there:
        @pl.when(present)
        def _(where=where):
            pl.semaphore_signal(barrier, inc=1, device_id=where, device_id_type=MESH)
        expected = expected + jnp.where(present, 1, 0)

    fine_own = (pl.ds(1, FL), pl.ds(8, 16), pl.ds(128, 256))
    coarse_own = (pl.ds(1, CL), pl.ds(8, 8), pl.ds(128, 128))
    loads = [
        (fine_now, qf.at[(pl.ds(0, 3), *fine_own)]),
        (fine_material.at[pl.ds(1, 3)], qf.at[(pl.ds(3, 3), *fine_own)]),
        (fine_before, qf.at[(pl.ds(6, 3), *fine_own)]),
        (fine_material.at[pl.ds(0, 1)], qf.at[(pl.ds(9, 1), *fine_own)]),
        (coarse_now, qc.at[(pl.ds(0, 3), *coarse_own)]),
        (coarse_material.at[pl.ds(1, 2)], qc.at[(pl.ds(3, 2), *coarse_own)]),
        (coarse_before, qc.at[(pl.ds(5, 3), *coarse_own)]),
        (coarse_material.at[pl.ds(0, 1)], qc.at[(pl.ds(8, 1), *coarse_own)]),
    ]
    copies = [pltpu.make_async_copy(src, dst, load_sem.at[k]) for k, (src, dst) in enumerate(loads)]
    for copy in copies:
        copy.start()

    def zero_unless(present, ref, at=None):
        @pl.when(jnp.logical_not(present))
        def _():
            if at is None:
                ref[...] = jnp.zeros(ref.shape, F32)
            else:
                ref[at] = jnp.zeros(ref.shape[1:], F32)

    zero_unless(there[0][1], rx_low)
    zero_unless(there[1][1], rx_high)
    for k in range(2):
        zero_unless(there[2 + k][1], ry, k)
    for k in range(4):
        zero_unless(there[4 + k][1], rc, k)

    @pl.when(top)
    def _():
        for c in range(3):
            qf[c, 0] = jnp.zeros((FR, FW), F32)
            u1f[c, 0] = jnp.zeros((FR, FW), F32)
        for k in range(3, 6):
            qf[k, 0] = jnp.zeros((FR, FW), F32)

    @pl.when(jnp.logical_not(top))
    def _():
        for c in range(3):
            qc[c, CL + 1] = jnp.zeros((CR, CW), F32)
            u1c[c, CL + 1] = jnp.zeros((CR, CW), F32)

    for copy in copies:
        copy.wait()
    for l in range(FL):
        own = (9, l + 1, pl.ds(8, 16), pl.ds(128, 256))
        qf[own] = STEP_SQUARED / qf[own]
    for l in range(CL):
        own = (8, l + 1, pl.ds(8, 8), pl.ds(128, 128))
        qc[own] = (0.25 * STEP_SQUARED) / qc[own]
    pack_x(qf, qc, sx_low, sx_high)
    pack_y(qf, qc, sy, sc)

    areas = (
        ((pl.ds(8, 16), pl.ds(128, 256)), (pl.ds(8, 8), pl.ds(128, 128)), ((1, 1),)),
        ((pl.ds(0, FR), pl.ds(0, 128)), (pl.ds(0, CR), pl.ds(0, 128)), ((0, 0), (1, 0))),
        ((pl.ds(0, 8), pl.ds(128, 256)), (pl.ds(0, 8), pl.ds(128, 128)), ((0, 1),)),
    )

    def deep_copy(src, dst, phase, k):
        return pltpu.make_async_remote_copy(
            src, dst, deep_send.at[phase, k], deep_recv.at[phase, k], device_id=partner, device_id_type=MESH
        )

    def restricted(phase, cur_f, places):
        @pl.when(jnp.logical_not(top))
        def _():
            for c in range(3):
                for r, w in places:
                    give[phase, c, 8 * r : 8 * r + 8, 128 * w : 128 * w + 128] = restrict(
                        lambda a, b: cur_f[c, FL, 8 * a : 8 * a + 8, 128 * b : 128 * b + 128], r, w
                    )

    from_top, from_bottom = [], []
    for part, (fine, coarse, _) in enumerate(areas):
        from_top.append(
            [
                deep_copy(qf.at[(pl.ds(0, 6), FL, *fine)], qf.at[(pl.ds(0, 6), 0, *fine)], 0, part * 3),
                deep_copy(qc.at[(pl.ds(0, 5), CL, *coarse)], qc.at[(pl.ds(0, 5), 0, *coarse)], 0, part * 3 + 1),
                deep_copy(qc.at[(pl.ds(0, 3), 1, *coarse)], got.at[(0, pl.ds(0, 3), *coarse)], 0, part * 3 + 2),
            ]
        )
        from_bottom.append(
            [
                deep_copy(qf.at[(pl.ds(0, 3), 1, *fine)], qf.at[(pl.ds(0, 3), FL + 1, *fine)], 0, part * 3),
                deep_copy(qc.at[(pl.ds(0, 3), 1, *coarse)], qc.at[(pl.ds(0, 3), CL + 1, *coarse)], 0, part * 3 + 1),
                deep_copy(give.at[(0, pl.ds(0, 3), *coarse)], qc.at[(pl.ds(0, 3), 0, *coarse)], 0, part * 3 + 2),
            ]
        )

    def start_part(part):
        @pl.when(top)
        def _():
            for copy in from_top[part]:
                copy.start()

        @pl.when(jnp.logical_not(top))
        def _():
            for copy in from_bottom[part]:
                copy.start()

    restricted(0, qf, areas[0][2])
    pl.semaphore_wait(barrier, expected)

    high_first, high_rest = pl.ds(0, X_HIGH_FIRST), pl.ds(X_HIGH_FIRST, X_REST)
    low_first, low_rest = pl.ds(0, X_LOW_FIRST), pl.ds(X_LOW_FIRST, X_REST)
    messages = [
        (0, sx_high.at[high_first], rx_high.at[high_first]), (1, sx_low.at[low_first], rx_low.at[low_first]),
        (2, sy, ry.at[1]), (3, sy, ry.at[0]),
        (4, sc.at[0], rc.at[3]), (5, sc.at[0], rc.at[2]), (6, sc.at[1], rc.at[1]), (7, sc.at[1], rc.at[0]),
        (0, sx_high.at[high_rest], rx_high.at[high_rest]), (1, sx_low.at[low_rest], rx_low.at[low_rest]),
    ]
    sends = []
    for n, (k, src, dst) in enumerate(messages):
        copy = pltpu.make_async_remote_copy(
            src, dst, send_sem.at[n], recv_sem.at[n], device_id=there[k][0], device_id_type=MESH
        )

        @pl.when(there[k][1])
        def _(copy=copy):
            copy.start()

        sends.append((k, copy))

    def arrived(*numbers):
        for n in numbers:
            k, copy = sends[n]
            opposite = SIDES.index((-SIDES[k][0], -SIDES[k][1]))

            @pl.when(there[opposite][1])
            def _(copy=copy):
                copy.wait_recv()

    start_part(0)
    arrived(2, 3, 4, 5, 6, 7)
    unpack_y(qf, qc, ry, rc)
    restricted(0, qf, areas[1][2])
    start_part(1)
    arrived(0, 1)
    unpack_x(qf, qc, rx_low, rx_high, True)
    restricted(0, qf, areas[2][2])
    start_part(2)

    @pl.when(top)
    def _():
        for k in range(3, 5):
            qc[k, 0] = qc[k, 1]

    arrived(8, 9)
    unpack_x(qf, qc, rx_low, rx_high, False)

    def prolonged(phase, cur_f):
        for c in range(3):
            large = prolong(lambda r, w: got[phase, c, 8 * r : 8 * r + 8, 128 * w : 128 * w + 128])
            for r in range(3):
                for w in range(3):
                    cur_f[c, FL + 1, 8 * r : 8 * r + 8, 128 * w : 128 * w + 128] = large[r][w]

    def keep_f(c, slot, value):
        u1f[c, slot] = value

    def keep_c(c, slot, value):
        u1c[c, slot] = value

    def out_f(c, slot, value):
        fine_out[c, slot - 1] = value

    def out_c(c, slot, value):
        coarse_out[c, slot - 1] = value

    first_f = Step(FL, qf, qf, lambda c, s: qf[6 + c, s], 9, True, keep_f, (0, 0))
    first_c = Step(CL, qc, qc, lambda c, s: qc[5 + c, s], 8, False, keep_c, (0, 0))
    second_f = Step(FL, u1f, qf, lambda c, s: qf[c, s], 9, True, out_f, (8, 128))
    second_c = Step(CL, u1c, qc, lambda c, s: qc[c, s], 8, False, out_c, (8, 128))

    first_f.inner()
    first_c.inner()

    @pl.when(top)
    def _():
        for part in from_bottom:
            for copy in part:
                copy.wait_recv()

    @pl.when(jnp.logical_not(top))
    def _():
        for part in from_top:
            for copy in part:
                copy.wait_recv()
        prolonged(0, qf)

    mine_f, theirs_f = jnp.where(top, FL, 1), jnp.where(top, 0, FL + 1)
    mine_c, theirs_c = jnp.where(top, CL, 1), jnp.where(top, 0, CL + 1)
    later_f = deep_copy(u1f.at[pl.ds(0, 3), mine_f], u1f.at[pl.ds(0, 3), theirs_f], 1, 0)
    later_c = deep_copy(u1c.at[pl.ds(0, 3), mine_c], u1c.at[pl.ds(0, 3), theirs_c], 1, 1)
    down = deep_copy(u1c.at[pl.ds(0, 3), 1], got.at[1], 1, 2)
    up = deep_copy(give.at[1], u1c.at[pl.ds(0, 3), 0], 1, 2)

    first_f.outer()
    later_f.start()
    restricted(1, u1f, ((0, 0), (0, 1), (1, 0), (1, 1)))

    @pl.when(jnp.logical_not(top))
    def _():
        up.start()

    first_c.outer()
    later_c.start()

    @pl.when(top)
    def _():
        down.start()

    second_f.inner()
    second_c.inner()
    later_f.wait_recv()
    later_c.wait_recv()

    @pl.when(top)
    def _():
        up.wait_recv()

    @pl.when(jnp.logical_not(top))
    def _():
        down.wait_recv()
        prolonged(1, u1f)

    second_f.outer()
    second_c.outer()

    later_f.wait_send()
    later_c.wait_send()

    @pl.when(top)
    def _():
        for copy in [copy for part in from_top for copy in part] + [down]:
            copy.wait_send()

    @pl.when(jnp.logical_not(top))
    def _():
        for copy in [copy for part in from_bottom for copy in part] + [up]:
            copy.wait_send()

    for k, copy in sends:
        @pl.when(there[k][1])
        def _(copy=copy):
            copy.wait_send()


def store(fine, coarse, fine_out, coarse_out, sems):
    copies = [pltpu.make_async_copy(fine, fine_out, sems.at[0]), pltpu.make_async_copy(coarse, coarse_out, sems.at[1])]
    for copy in copies:
        copy.start()
    for copy in copies:
        copy.wait()


def per_device(*arrays):
    fine, coarse = arrays[0], arrays[3]
    after = stepped(arrays, fine, coarse)
    return pl.pallas_call(
        store,
        out_shape=(jax.ShapeDtypeStruct(fine.shape, F32), jax.ShapeDtypeStruct(coarse.shape, F32)),
        in_specs=[pl.BlockSpec(memory_space=pltpu.VMEM)] * 2,
        out_specs=(pl.BlockSpec(memory_space=pltpu.HBM), pl.BlockSpec(memory_space=pltpu.HBM)),
        scratch_shapes=[pltpu.SemaphoreType.DMA((2,))],
    )(*[pltpu.with_memory_space_constraint(a, pltpu.VMEM) for a in after])


def stepped(arrays, fine, coarse):
    return pl.pallas_call(
        kernel,
        out_shape=(pltpu.VMEM(fine.shape, F32), pltpu.VMEM(coarse.shape, F32)),
        in_specs=[pl.BlockSpec(memory_space=pltpu.HBM)] * 6,
        out_specs=(pl.BlockSpec(memory_space=pltpu.VMEM), pl.BlockSpec(memory_space=pltpu.VMEM)),
        scratch_shapes=[
            pltpu.VMEM((FQ, FL + 2, FR, FW), F32),
            pltpu.VMEM((CQ, CL + 2, CR, CW), F32),
            pltpu.VMEM((3, FL + 2, FR, FW), F32),
            pltpu.VMEM((3, CL + 2, CR, CW), F32),
            pltpu.VMEM((X_LOW_ROWS, 128), F32),
            pltpu.VMEM((X_ROWS, 128), F32),
            pltpu.VMEM((Y_ROWS, 128), F32),
            pltpu.VMEM((2, C_ROWS, 128), F32),
            pltpu.VMEM((X_LOW_ROWS, 128), F32),
            pltpu.VMEM((X_ROWS, 128), F32),
            pltpu.VMEM((2, Y_ROWS, 128), F32),
            pltpu.VMEM((4, C_ROWS, 128), F32),
            pltpu.VMEM((STEPS, 3, CR, CW), F32),
            pltpu.VMEM((STEPS, 3, CR, CW), F32),
            pltpu.SemaphoreType.DMA((8,)),
            pltpu.SemaphoreType.DMA((10,)),
            pltpu.SemaphoreType.DMA((10,)),
            pltpu.SemaphoreType.DMA((STEPS, 9)),
            pltpu.SemaphoreType.DMA((STEPS, 9)),
        ],
        compiler_params=pltpu.CompilerParams(
            collective_id=0, has_side_effects=True, vmem_limit_bytes=40 * 2**20
        ),
    )(*[pltpu.with_memory_space_constraint(a, pltpu.HBM) for a in arrays])


def solution(mesh):
    spec = P(None, "dev", "gx", "gy")
    return jax.shard_map(
        per_device, mesh=mesh, in_specs=(spec,) * 6, out_specs=(spec, spec), check_vma=False
    )
```

```python
import jax
import jax.numpy as jnp
from jax import lax
from jax.experimental import pallas as pl
from jax.experimental.pallas import tpu as pltpu
from jax.sharding import PartitionSpec as P

STEPS = 2
STEP_SQUARED = 0.15 * 0.15
MESH = pl.DeviceIdType.MESH
F32 = jnp.float32

FR, FW = 24, 384
CR, CW = 16, 256
FL, CL = 4, 8
FQ = 10
CQ = 9

X_COARSE = 6 * 16
X_MEDIUM = X_COARSE + 6 * 8
X_EXTRA = X_MEDIUM + 2 * 8
X_LOW_FIRST = X_COARSE + 10 * 8
X_HIGH_FIRST = X_EXTRA + 2 * 16
X_REST = 4 * 16 + 4 * 8
X_LOW_REST = 2 * 16 + 4 * 8
X_LOW_ROWS = X_LOW_FIRST + X_LOW_REST
X_ROWS = X_HIGH_FIRST + X_REST
Y_FINE = 32
Y_COARSE = 24
Y_ROWS = Y_FINE + Y_COARSE
C_ROWS = 16
SIDES = ((-1, 0), (1, 0), (0, -1), (0, 1), (-1, -1), (-1, 1), (1, -1), (1, 1))


def iota(shape, dim):
    return lax.broadcasted_iota(jnp.int32, shape, dim)


def turned(value, shift, axis):
    shift = shift % value.shape[axis]
    return pltpu.roll(value, shift, axis) if shift else value


def picked(tile, index, axis):
    return jnp.take_along_axis(tile, index, axis=axis)


def restrict(tiles, r, w):
    row, lane = iota((8, 128), 0), iota((8, 128), 1)
    row_at, lane_at = (2 * row) & 7, (2 * lane) & 127

    def pairs(tile, axis, at):
        return picked(tile + turned(tile, -1, axis), at, axis)

    def joined(values, half, at):
        return values[0] if len(values) == 1 else jnp.where(at < half, values[0], values[1])

    sources = ((0,), (1, 2))
    columns = [joined([pairs(tiles(a, b), 0, row_at) for a in sources[r]], 4, row) for b in sources[w]]
    return joined([0.25 * pairs(v, 1, lane_at) for v in columns], 64, lane)


def prolong(tiles):
    row, lane = iota((8, 128), 0), iota((8, 128), 1)

    def spread(halo, own, half, at, axis):
        low = at // 2
        return (
            picked(halo, jnp.where(at < half, low, low + half), axis),
            picked(own, low, axis),
            picked(own, low + half, axis),
        )

    rows = [spread(tiles(r, 0), tiles(r, 1), 64, lane, 1) for r in range(2)]
    columns = [spread(rows[0][w], rows[1][w], 4, row, 0) for w in range(3)]
    return [[columns[w][r] for w in range(3)] for r in range(3)]


def gradients_to_stress(here, below, medium, stretch, which):
    def ahead(value, axis):
        return turned(value, -1, axis)

    mu, lam = medium
    dz = [b - h for b, h in zip(below, here)]
    if stretch is not None:
        dz = [d * stretch for d in dz]
    dx = [ahead(h, 0) - h for h in here]
    dy = [ahead(h, 1) - h for h in here]
    bulk = lam * (dx[0] + dy[1] + dz[2])
    twice = mu + mu
    out = {"zz": bulk + twice * dz[2], "xz": mu * (dz[0] + dx[2]), "yz": mu * (dz[1] + dy[2])}
    if which == "all":
        out["xx"] = bulk + twice * dx[0]
        out["yy"] = bulk + twice * dy[1]
        out["xy"] = mu * (dy[0] + dx[1])
    return out


class Step:
    def __init__(self, count, cur, qty, before_at, scale_at, stretched, write, crop):
        self.count, self.cur, self.qty, self.before_at = count, cur, qty, before_at
        self.scale_at, self.stretched, self.write, self.crop = scale_at, stretched, write, crop

    def cut(self, value):
        return value[self.crop[0] :, self.crop[1] :]

    def stress(self, slot, which="all"):
        cur, qty = self.cur, self.qty
        stretch = qty[5, slot] if self.stretched else None
        return gradients_to_stress(
            [cur[c, slot] for c in range(3)],
            [cur[c, slot + 1] for c in range(3)],
            (qty[3, slot], qty[4, slot]),
            stretch,
            which,
        )

    def move(self, slot, s, above):
        cut = self.cut

        def back_x(name):
            return cut(s[name]) - cut(turned(s[name], 1, 0))

        def back_y(name):
            return cut(s[name]) - cut(turned(s[name], 1, 1))

        def back_z(name):
            d = cut(s[name]) - cut(above[name])
            return d * cut(self.qty[5, slot]) if self.stretched else d

        force = (
            back_x("xx") + back_y("xy") + back_z("xz"),
            back_x("xy") + back_y("yy") + back_z("yz"),
            back_x("xz") + back_y("yz") + back_z("zz"),
        )
        scale = cut(self.qty[self.scale_at, slot])
        for c in range(3):
            now = cut(self.cur[c, slot])
            before = cut(self.before_at(c, slot))
            self.write(c, slot, now + now - before + scale * force[c])

    def inner(self):
        self.first = above = self.stress(1)
        for slot in range(2, self.count):
            s = self.stress(slot)
            self.move(slot, s, above)
            above = s
        self.above = above

    def outer(self):
        last = self.stress(self.count)
        self.move(self.count, last, self.above)
        self.move(1, self.first, self.stress(0, "vertical"))


def fine_at(g, first):
    return g * 16 if g < 6 else first + (g - 6) * 16


def pack_x(qf, qc, low, high):
    row8 = iota((8, 256), 0)
    crow = iota((8, 128), 0)

    def store(ref, at, value):
        ref[pl.ds(at, 8), :] = value[:, :128]
        ref[pl.ds(at + 8, 8), :] = value[:, 128:]

    for g in range(FQ):
        up = jnp.zeros((8, 256), F32)
        down = up
        for l in range(FL):
            z = jnp.where(row8 < 4, qf[g, l + 1, 8:16, 128:], qf[g, l + 1, 16:24, 128:])
            t = turned(z, 2 * l, 0)
            up = t if l == 0 else jnp.where(row8 // 2 == l, t, up)
            down = t if l == 0 else jnp.where(row8 // 2 == l - 1, t, down)
        store(high, fine_at(g, X_HIGH_FIRST), up)
        if g < 6:
            store(low, g * 16, down)
    for pair in range(2):
        for k in range(8):
            t = turned(qf[6 + 2 * pair + k // 4, k % 4 + 1, 16:24, 128:], k, 0)
            down = t if k == 0 else jnp.where(row8 == k - 1, t, down)
        store(low, X_LOW_FIRST + pair * 16, down)
    for q in range(5):
        for half in range(2):
            for l in range(4):
                t = turned(qc[q, half * 4 + l + 1, 8:16, 128:], 2 * l, 0)
                up = t if l == 0 else jnp.where(crow // 2 == l, t, up)
                down = t if l == 0 else jnp.where(crow // 2 == l - 1, t, down)
            at = X_COARSE + (q * 2 + half) * 8
            if q < 3:
                high[pl.ds(at, 8), :] = up
            low[pl.ds(at, 8), :] = down
    for q in range(3, 5):
        for l in range(8):
            t = turned(qc[q, l + 1, 8:16, 128:], l, 0)
            up = t if l == 0 else jnp.where(crow == l, t, up)
        high[pl.ds(X_MEDIUM + (q - 3) * 8, 8), :] = up
    for q in range(4):
        for l in range(8):
            t = turned(qc[5 + q, l + 1, 8:16, 128:], l, 0)
            up = t if l == 0 else jnp.where(crow == l, t, up)
            down = t if l == 0 else jnp.where(crow == l - 1, t, down)
        high[pl.ds(X_HIGH_FIRST + 64 + q * 8, 8), :] = up
        low[pl.ds(X_LOW_FIRST + 32 + q * 8, 8), :] = down
    more = [jnp.where(row8 < 2, turned(qf[c, 3, 8:16, 128:], -2, 0), qf[c, 4, 8:16, 128:]) for c in range(3)]
    store(high, X_EXTRA, jnp.where(row8 < 4, more[0], turned(more[1], 4, 0)))
    store(high, X_EXTRA + 16, more[2])


def unpack_x(qf, qc, low, high, first):
    row8 = iota((8, 256), 0)
    crow = iota((8, 128), 0)

    def load(ref, at):
        return jnp.concatenate([ref[pl.ds(at, 8), :], ref[pl.ds(at + 8, 8), :]], axis=1)

    for g in range(6) if first else range(6, FQ):
        up = load(high, fine_at(g, X_HIGH_FIRST))
        down = load(low, g * 16 if g < 6 else X_LOW_FIRST + (g - 6) // 2 * 16)
        more = turned(load(high, X_EXTRA + g // 2 * 16), -4 * (g % 2), 0) if g < 3 else None
        for l in range(FL):
            back = 2 * l if g < 6 else (g - 6) % 2 * 4 + l
            t = jnp.where(row8 < 4, turned(up, -2 * l, 0), turned(down, -back, 0))
            if g < 3 and l == 2:
                t = jnp.where(row8 // 2 == 1, turned(more, 2, 0), t)
            if g < 3 and l == 3:
                t = jnp.where(row8 // 2 == 1, more, t)
            qf[g, l + 1, 0:8, 128:] = t
    for q in range(5) if first else ():
        for half in range(2):
            at = X_COARSE + (q * 2 + half) * 8
            up = high[pl.ds(at if q < 3 else X_MEDIUM + (q - 3) * 8, 8), :]
            down = low[pl.ds(at, 8), :]
            for l in range(4):
                shift = 2 * l if q < 3 else half * 4 + l
                t = jnp.where(crow < 4, turned(up, -shift, 0), turned(down, -2 * l, 0))
                qc[q, half * 4 + l + 1, 0:8, 128:] = t
    for q in () if first else range(4):
        up = high[pl.ds(X_HIGH_FIRST + 64 + q * 8, 8), :]
        down = low[pl.ds(X_LOW_FIRST + 32 + q * 8, 8), :]
        for l in range(8):
            qc[5 + q, l + 1, 0:8, 128:] = jnp.where(crow < 4, turned(up, -l, 0), turned(down, -l, 0))


def pack_y(qf, qc, out, corner):
    lane = iota((16, 128), 1)
    lane8 = iota((8, 128), 1)
    row8 = iota((8, 128), 0)
    fine, coarse = [], []
    for t in range(2):
        packed = jnp.zeros((16, 128), F32)
        for k in range(20):
            g, l = t * 5 + k // 4, k % 4
            z = jnp.where(lane < 64, qf[g, l + 1, 8:24, 128:256], qf[g, l + 1, 8:24, 256:384])
            mine = ((lane + (2 - 6 * k + 128)) & 127) < 6
            packed = jnp.where(mine, turned(z, 6 * k, 1), packed)
        out[pl.ds(t * 16, 16), :] = packed
        fine.append(packed)
    for t in range(3):
        packed = jnp.zeros((8, 128), F32)
        for k in range(32 if t < 2 else 8):
            q, l = t * 4 + k // 8, k % 8
            mine = ((lane8 + (2 - 4 * k + 128)) & 127) < 4
            packed = jnp.where(mine, turned(qc[q, l + 1, 8:16, 128:256], 4 * k, 1), packed)
        out[pl.ds(Y_FINE + t * 8, 8), :] = packed
        coarse.append(packed)
    corner[0, 0:8] = jnp.where(row8 < 4, fine[0][:8], turned(fine[1][:8], 4, 0))
    corner[0, 8:16] = jnp.where(
        row8 < 2, coarse[0], jnp.where(row8 < 4, turned(coarse[1], 2, 0), turned(coarse[2], 4, 0))
    )
    corner[1, 0:8] = jnp.where(row8 >= 6, fine[0][8:], turned(fine[1][8:], -2, 0))
    corner[1, 8:16] = jnp.where(
        row8 >= 6, coarse[0], jnp.where(row8 >= 4, turned(coarse[1], -2, 0), turned(coarse[2], -4, 0))
    )


def unpack_y(qf, qc, side, corner):
    lane = iota((16, 128), 1)
    lane8 = iota((8, 128), 1)
    row8 = iota((8, 128), 0)
    fine_low = ((lane + 2) & 127) % 6 < 2
    fine_low8 = ((lane8 + 2) & 127) % 6 < 2
    coarse_low8 = ((lane8 + 2) & 127) % 4 < 2

    def corners(at, low, up, down):
        before = jnp.where(low, corner[0, at : at + 8], corner[1, at : at + 8])
        after = jnp.where(low, corner[2, at : at + 8], corner[3, at : at + 8])
        return jnp.where(row8 < 4, turned(after, up, 0), turned(before, down, 0))

    for t in range(2):
        own = jnp.where(fine_low, side[0, pl.ds(t * 16, 16), :], side[1, pl.ds(t * 16, 16), :])
        both = jnp.concatenate([corners(0, fine_low8, -4 * t, 2 * t), own], axis=0)
        for k in range(20):
            g, l = t * 5 + k // 4, k % 4
            qf[g, l + 1, :, 0:128] = turned(both, -6 * k, 1)
    for t in range(3):
        at = Y_FINE + t * 8
        own = jnp.where(coarse_low8, side[0, pl.ds(at, 8), :], side[1, pl.ds(at, 8), :])
        both = jnp.concatenate([corners(8, coarse_low8, -2 * t, 2 * t), own], axis=0)
        for k in range(32 if t < 2 else 8):
            q, l = t * 4 + k // 8, k % 8
            qc[q, l + 1, :, 0:128] = turned(both, -4 * k, 1)


def kernel(
    fine_now, fine_before, fine_material, coarse_now, coarse_before, coarse_material,
    fine_out, coarse_out,
    qf, qc, u1f, u1c,
    sx_low, sx_high, sy, sc, rx_low, rx_high, ry, rc,
    give, got,
    load_sem, send_sem, recv_sem, deep_send, deep_recv,
):
    gx, gy, dev = lax.axis_index("gx"), lax.axis_index("gy"), lax.axis_index("dev")
    nx, ny = lax.axis_size("gx"), lax.axis_size("gy")
    top = dev == 0
    partner = {"gx": gx, "gy": gy, "dev": 1 - dev}
    there = []
    for dx, dy in SIDES:
        x, y = gx + dx, gy + dy
        there.append(({"gx": x, "gy": y, "dev": dev}, (x >= 0) & (x < nx) & (y >= 0) & (y < ny)))

    barrier = pltpu.get_barrier_semaphore()
    expected = 1
    pl.semaphore_signal(barrier, inc=1, device_id=partner, device_id_type=MESH)
    for where, present in there:
        @pl.when(present)
        def _(where=where):
            pl.semaphore_signal(barrier, inc=1, device_id=where, device_id_type=MESH)
        expected = expected + jnp.where(present, 1, 0)

    fine_own = (pl.ds(1, FL), pl.ds(8, 16), pl.ds(128, 256))
    coarse_own = (pl.ds(1, CL), pl.ds(8, 8), pl.ds(128, 128))
    loads = [
        (fine_now, qf.at[(pl.ds(0, 3), *fine_own)]),
        (fine_material.at[pl.ds(1, 3)], qf.at[(pl.ds(3, 3), *fine_own)]),
        (fine_before, qf.at[(pl.ds(6, 3), *fine_own)]),
        (fine_material.at[pl.ds(0, 1)], qf.at[(pl.ds(9, 1), *fine_own)]),
        (coarse_now, qc.at[(pl.ds(0, 3), *coarse_own)]),
        (coarse_material.at[pl.ds(1, 2)], qc.at[(pl.ds(3, 2), *coarse_own)]),
        (coarse_before, qc.at[(pl.ds(5, 3), *coarse_own)]),
        (coarse_material.at[pl.ds(0, 1)], qc.at[(pl.ds(8, 1), *coarse_own)]),
    ]
    copies = [pltpu.make_async_copy(src, dst, load_sem.at[k]) for k, (src, dst) in enumerate(loads)]
    for copy in copies:
        copy.start()

    def zero_unless(present, ref, at=None):
        @pl.when(jnp.logical_not(present))
        def _():
            if at is None:
                ref[...] = jnp.zeros(ref.shape, F32)
            else:
                ref[at] = jnp.zeros(ref.shape[1:], F32)

    zero_unless(there[0][1], rx_low)
    zero_unless(there[1][1], rx_high)
    for k in range(2):
        zero_unless(there[2 + k][1], ry, k)
    for k in range(4):
        zero_unless(there[4 + k][1], rc, k)

    @pl.when(top)
    def _():
        for c in range(3):
            qf[c, 0] = jnp.zeros((FR, FW), F32)
            u1f[c, 0] = jnp.zeros((FR, FW), F32)
        for k in range(3, 6):
            qf[k, 0] = jnp.zeros((FR, FW), F32)

    @pl.when(jnp.logical_not(top))
    def _():
        for c in range(3):
            qc[c, CL + 1] = jnp.zeros((CR, CW), F32)
            u1c[c, CL + 1] = jnp.zeros((CR, CW), F32)

    for copy in copies:
        copy.wait()
    for l in range(FL):
        own = (9, l + 1, pl.ds(8, 16), pl.ds(128, 256))
        qf[own] = STEP_SQUARED / qf[own]
    for l in range(CL):
        own = (8, l + 1, pl.ds(8, 8), pl.ds(128, 128))
        qc[own] = (0.25 * STEP_SQUARED) / qc[own]
    pack_x(qf, qc, sx_low, sx_high)
    pack_y(qf, qc, sy, sc)

    areas = (
        ((pl.ds(8, 16), pl.ds(128, 256)), (pl.ds(8, 8), pl.ds(128, 128)), ((1, 1),)),
        ((pl.ds(0, FR), pl.ds(0, 128)), (pl.ds(0, CR), pl.ds(0, 128)), ((0, 0), (1, 0))),
        ((pl.ds(0, 8), pl.ds(128, 256)), (pl.ds(0, 8), pl.ds(128, 128)), ((0, 1),)),
    )

    def deep_copy(src, dst, phase, k):
        return pltpu.make_async_remote_copy(
            src, dst, deep_send.at[phase, k], deep_recv.at[phase, k], device_id=partner, device_id_type=MESH
        )

    def restricted(phase, cur_f, places):
        @pl.when(jnp.logical_not(top))
        def _():
            for c in range(3):
                for r, w in places:
                    give[phase, c, 8 * r : 8 * r + 8, 128 * w : 128 * w + 128] = restrict(
                        lambda a, b: cur_f[c, FL, 8 * a : 8 * a + 8, 128 * b : 128 * b + 128], r, w
                    )

    from_top, from_bottom = [], []
    for part, (fine, coarse, _) in enumerate(areas):
        from_top.append(
            [
                deep_copy(qf.at[(pl.ds(0, 6), FL, *fine)], qf.at[(pl.ds(0, 6), 0, *fine)], 0, part * 3),
                deep_copy(qc.at[(pl.ds(0, 5), CL, *coarse)], qc.at[(pl.ds(0, 5), 0, *coarse)], 0, part * 3 + 1),
                deep_copy(qc.at[(pl.ds(0, 3), 1, *coarse)], got.at[(0, pl.ds(0, 3), *coarse)], 0, part * 3 + 2),
            ]
        )
        from_bottom.append(
            [
                deep_copy(qf.at[(pl.ds(0, 3), 1, *fine)], qf.at[(pl.ds(0, 3), FL + 1, *fine)], 0, part * 3),
                deep_copy(qc.at[(pl.ds(0, 3), 1, *coarse)], qc.at[(pl.ds(0, 3), CL + 1, *coarse)], 0, part * 3 + 1),
                deep_copy(give.at[(0, pl.ds(0, 3), *coarse)], qc.at[(pl.ds(0, 3), 0, *coarse)], 0, part * 3 + 2),
            ]
        )

    def start_part(part):
        @pl.when(top)
        def _():
            for copy in from_top[part]:
                copy.start()

        @pl.when(jnp.logical_not(top))
        def _():
            for copy in from_bottom[part]:
                copy.start()

    restricted(0, qf, areas[0][2])
    pl.semaphore_wait(barrier, expected)

    high_first, high_rest = pl.ds(0, X_HIGH_FIRST), pl.ds(X_HIGH_FIRST, X_REST)
    low_first, low_rest = pl.ds(0, X_LOW_FIRST), pl.ds(X_LOW_FIRST, X_LOW_REST)
    messages = [
        (0, sx_high.at[high_first], rx_high.at[high_first]), (1, sx_low.at[low_first], rx_low.at[low_first]),
        (2, sy, ry.at[1]), (3, sy, ry.at[0]),
        (4, sc.at[0], rc.at[3]), (5, sc.at[0], rc.at[2]), (6, sc.at[1], rc.at[1]), (7, sc.at[1], rc.at[0]),
        (0, sx_high.at[high_rest], rx_high.at[high_rest]), (1, sx_low.at[low_rest], rx_low.at[low_rest]),
    ]
    sends = []
    for n, (k, src, dst) in enumerate(messages):
        copy = pltpu.make_async_remote_copy(
            src, dst, send_sem.at[n], recv_sem.at[n], device_id=there[k][0], device_id_type=MESH
        )

        @pl.when(there[k][1])
        def _(copy=copy):
            copy.start()

        sends.append((k, copy))

    def arrived(*numbers):
        for n in numbers:
            k, copy = sends[n]
            opposite = SIDES.index((-SIDES[k][0], -SIDES[k][1]))

            @pl.when(there[opposite][1])
            def _(copy=copy):
                copy.wait_recv()

    start_part(0)
    arrived(2, 3, 4, 5, 6, 7)
    unpack_y(qf, qc, ry, rc)
    restricted(0, qf, areas[1][2])
    start_part(1)
    arrived(0, 1)
    unpack_x(qf, qc, rx_low, rx_high, True)
    restricted(0, qf, areas[2][2])
    start_part(2)

    @pl.when(top)
    def _():
        for k in range(3, 5):
            qc[k, 0] = qc[k, 1]

    arrived(8, 9)
    unpack_x(qf, qc, rx_low, rx_high, False)

    def prolonged(phase, cur_f):
        for c in range(3):
            large = prolong(lambda r, w: got[phase, c, 8 * r : 8 * r + 8, 128 * w : 128 * w + 128])
            for r in range(3):
                for w in range(3):
                    cur_f[c, FL + 1, 8 * r : 8 * r + 8, 128 * w : 128 * w + 128] = large[r][w]

    def keep_f(c, slot, value):
        u1f[c, slot] = value

    def keep_c(c, slot, value):
        u1c[c, slot] = value

    def out_f(c, slot, value):
        fine_out[c, slot - 1] = value

    def out_c(c, slot, value):
        coarse_out[c, slot - 1] = value

    first_f = Step(FL, qf, qf, lambda c, s: qf[6 + c, s], 9, True, keep_f, (0, 0))
    first_c = Step(CL, qc, qc, lambda c, s: qc[5 + c, s], 8, False, keep_c, (0, 0))
    second_f = Step(FL, u1f, qf, lambda c, s: qf[c, s], 9, True, out_f, (8, 128))
    second_c = Step(CL, u1c, qc, lambda c, s: qc[c, s], 8, False, out_c, (8, 128))

    first_f.inner()
    first_c.inner()

    @pl.when(top)
    def _():
        for part in from_bottom:
            for copy in part:
                copy.wait_recv()

    @pl.when(jnp.logical_not(top))
    def _():
        for part in from_top:
            for copy in part:
                copy.wait_recv()
        prolonged(0, qf)

    mine_f, theirs_f = jnp.where(top, FL, 1), jnp.where(top, 0, FL + 1)
    mine_c, theirs_c = jnp.where(top, CL, 1), jnp.where(top, 0, CL + 1)
    later_f = deep_copy(u1f.at[pl.ds(0, 3), mine_f], u1f.at[pl.ds(0, 3), theirs_f], 1, 0)
    later_c = deep_copy(u1c.at[pl.ds(0, 3), mine_c], u1c.at[pl.ds(0, 3), theirs_c], 1, 1)
    down = deep_copy(u1c.at[pl.ds(0, 3), 1], got.at[1], 1, 2)
    up = deep_copy(give.at[1], u1c.at[pl.ds(0, 3), 0], 1, 2)

    first_f.outer()
    later_f.start()
    restricted(1, u1f, ((0, 0), (0, 1), (1, 0), (1, 1)))

    @pl.when(jnp.logical_not(top))
    def _():
        up.start()

    first_c.outer()
    later_c.start()

    @pl.when(top)
    def _():
        down.start()

    second_f.inner()
    second_c.inner()
    later_f.wait_recv()
    later_c.wait_recv()

    @pl.when(top)
    def _():
        up.wait_recv()

    @pl.when(jnp.logical_not(top))
    def _():
        down.wait_recv()
        prolonged(1, u1f)

    second_f.outer()
    second_c.outer()

    later_f.wait_send()
    later_c.wait_send()

    @pl.when(top)
    def _():
        for copy in [copy for part in from_top for copy in part] + [down]:
            copy.wait_send()

    @pl.when(jnp.logical_not(top))
    def _():
        for copy in [copy for part in from_bottom for copy in part] + [up]:
            copy.wait_send()

    for k, copy in sends:
        @pl.when(there[k][1])
        def _(copy=copy):
            copy.wait_send()


def store(fine, coarse, fine_out, coarse_out, sems):
    copies = [pltpu.make_async_copy(fine, fine_out, sems.at[0]), pltpu.make_async_copy(coarse, coarse_out, sems.at[1])]
    for copy in copies:
        copy.start()
    for copy in copies:
        copy.wait()


def per_device(*arrays):
    fine, coarse = arrays[0], arrays[3]
    after = stepped(arrays, fine, coarse)
    return pl.pallas_call(
        store,
        out_shape=(jax.ShapeDtypeStruct(fine.shape, F32), jax.ShapeDtypeStruct(coarse.shape, F32)),
        in_specs=[pl.BlockSpec(memory_space=pltpu.VMEM)] * 2,
        out_specs=(pl.BlockSpec(memory_space=pltpu.HBM), pl.BlockSpec(memory_space=pltpu.HBM)),
        scratch_shapes=[pltpu.SemaphoreType.DMA((2,))],
    )(*[pltpu.with_memory_space_constraint(a, pltpu.VMEM) for a in after])


def stepped(arrays, fine, coarse):
    return pl.pallas_call(
        kernel,
        out_shape=(pltpu.VMEM(fine.shape, F32), pltpu.VMEM(coarse.shape, F32)),
        in_specs=[pl.BlockSpec(memory_space=pltpu.HBM)] * 6,
        out_specs=(pl.BlockSpec(memory_space=pltpu.VMEM), pl.BlockSpec(memory_space=pltpu.VMEM)),
        scratch_shapes=[
            pltpu.VMEM((FQ, FL + 2, FR, FW), F32),
            pltpu.VMEM((CQ, CL + 2, CR, CW), F32),
            pltpu.VMEM((3, FL + 2, FR, FW), F32),
            pltpu.VMEM((3, CL + 2, CR, CW), F32),
            pltpu.VMEM((X_LOW_ROWS, 128), F32),
            pltpu.VMEM((X_ROWS, 128), F32),
            pltpu.VMEM((Y_ROWS, 128), F32),
            pltpu.VMEM((2, C_ROWS, 128), F32),
            pltpu.VMEM((X_LOW_ROWS, 128), F32),
            pltpu.VMEM((X_ROWS, 128), F32),
            pltpu.VMEM((2, Y_ROWS, 128), F32),
            pltpu.VMEM((4, C_ROWS, 128), F32),
            pltpu.VMEM((STEPS, 3, CR, CW), F32),
            pltpu.VMEM((STEPS, 3, CR, CW), F32),
            pltpu.SemaphoreType.DMA((8,)),
            pltpu.SemaphoreType.DMA((10,)),
            pltpu.SemaphoreType.DMA((10,)),
            pltpu.SemaphoreType.DMA((STEPS, 9)),
            pltpu.SemaphoreType.DMA((STEPS, 9)),
        ],
        compiler_params=pltpu.CompilerParams(
            collective_id=0, has_side_effects=True, vmem_limit_bytes=40 * 2**20
        ),
    )(*[pltpu.with_memory_space_constraint(a, pltpu.HBM) for a in arrays])


def solution(mesh):
    spec = P(None, "dev", "gx", "gy")
    return jax.shard_map(
        per_device, mesh=mesh, in_specs=(spec,) * 6, out_specs=(spec, spec), check_vma=False
    )
```
